32 devices in a mesh: slab: 16 (over z, y, x), bal: 2 (over core).
Axes of the slice: x: 2, y: 2, z: 4, core: 2. Of those that a mesh axis runs over, the one named last changes fastest.
Arguments:
- order_parameter: float32 [16, 4, 32, 1024], P('slab', 'bal'), may hold values from -1 to 1
- concentration_excess: float32 [16, 4, 32, 1024], P('slab', 'bal'), may hold values from -1.8 to 1.8
- thermal_subcooling: float32 [16, 4, 32, 1024], P('slab', 'bal'), may hold values from -1.8 to 1.8
- holder_places_prior: int32 [16, 4], replicated, may hold values from 0 to 3, as said below
- holder_places_revised: int32 [16, 4], replicated, may hold values from 0 to 3, as said below
- update_flags: int32 [16, 4], replicated, may hold values 0 or 1
Outputs:
- phase_out: float32 [16, 4, 32, 1024], P('slab', 'bal')
- solute_out: float32 [16, 4, 32, 1024], P('slab', 'bal')
- temperature_out: float32 [16, 4, 32, 1024], P('slab', 'bal')
The draws below stay inside these ranges and needn't reach their ends.
Inputs may be any that keep to these rules, and one draw needn't show every extreme that they name: `holder_places_prior`: each row is a permutation of the 4 positions of a layer; slot k belongs to the owner of index k // 2 along bal. `holder_places_revised`: each row is a permutation of the layer's positions. In every layer each owner gives exactly 1 of its blocks to other owners and receives exactly 1; every other block keeps its slot.
All inputs are finite; a program needn't handle non-finite values.
Results may differ from the reference program's by a relative error of at most 0.00002.
Values sent between devices are 32-bit elements; how exact they have to be, the bound alone decides.
No kernel may reach another device: no remote copies, remote signals or barrier semaphores. Data moves between devices by JAX's collectives and lax.ppermute only.
A program may use at most 64 MiB of HBM per device.

```python
import jax
import jax.numpy as jnp

TILE_SIDE_POINTS = 32
BZ = 4
BLK_DEV = 2
STEPS = 1
SHEET_COUNT = 16
TILES_IN_SHEET = 4
BY = 1
MOVE = 1


def small_permutation(sub_key):
    return jax.random.permutation(sub_key, BLK_DEV)


def layer_slots(layer_key):
    devices = TILES_IN_SHEET // BLK_DEV
    key_perm, key_rank, key_cycle = jax.random.split(layer_key, 3)
    before = jax.random.permutation(key_perm, TILES_IN_SHEET).astype(jnp.int32)
    ranks = jax.vmap(small_permutation)(jax.random.split(key_rank, devices))
    slot_of_rank = jnp.argsort(ranks, axis=1).astype(jnp.int32)
    after = before
    cycle_keys = jax.random.split(key_cycle, MOVE)
    for turn in range(MOVE):
        order = jax.random.permutation(cycle_keys[turn], devices).astype(jnp.int32)
        place = jnp.argsort(order).astype(jnp.int32)
        target = order[(place + 1) % devices]
        source_slots = jnp.arange(devices, dtype=jnp.int32) * BLK_DEV + slot_of_rank[:, turn]
        target_slots = target * BLK_DEV + slot_of_rank[target, turn]
        after = after.at[target_slots].set(before[source_slots])
    return (before, after)


def shared_slots(key):
    base = jax.random.fold_in(key, 7)
    return jax.vmap(layer_slots)(jax.random.split(base, SHEET_COUNT))


def draw_holder_places_prior(key, part):
    return shared_slots(key)[0]


def draw_holder_places_revised(key, part):
    return shared_slots(key)[1]


def set_ends(array, key, smallest, largest):
    longest = array.shape.index(max(array.shape))
    spots = []
    for shift in (0, 1):
        where = [jax.random.randint(jax.random.fold_in(key, axis), (), 0, length) for axis, length in enumerate(array.shape)]
        where[longest] = (where[longest] + shift) % array.shape[longest]
        spots.append(tuple(where))
    return array.at[spots[0]].set(smallest).at[spots[1]].set(largest)


def block_scale(rng, extent, pieces, low, top_value):
    level = 1.0
    for dim, parts in pieces:
        steps = jax.random.uniform(jax.random.fold_in(jax.random.fold_in(rng, 6), dim), (parts,), jnp.float32, low / len(pieces), top_value / len(pieces))
        level = level * jnp.repeat(jnp.exp(steps), extent[dim] // parts).reshape((-1,) + (1,) * (len(extent) - 1 - dim))
    return level


def bell_draw(stream_key, extent, width, most, pieces=(), kind=jnp.bfloat16):
    loudness = block_scale(stream_key, extent, pieces, -0.22, 0.18) if pieces else 1.0
    entries = jax.random.normal(stream_key, extent, jnp.float32) * width * loudness
    return jnp.minimum(jnp.maximum(entries, -most), most).astype(kind)


def setup_inputs(seed: int = 0) -> dict:
    key_list = jax.random.split(jax.random.key(seed), 7)
    return {
        "order_parameter": jnp.clip(jax.random.uniform(key_list[0], (SHEET_COUNT, TILES_IN_SHEET, TILE_SIDE_POINTS, TILE_SIDE_POINTS * TILE_SIDE_POINTS), jnp.float32, -1.0, 1.0) * block_scale(key_list[0], (SHEET_COUNT, TILES_IN_SHEET, TILE_SIDE_POINTS, TILE_SIDE_POINTS * TILE_SIDE_POINTS), ((0, 16), (1, 2)), -0.4, 0.0), -1.0, 1.0),
        "concentration_excess": bell_draw(key_list[1], (SHEET_COUNT, TILES_IN_SHEET, TILE_SIDE_POINTS, TILE_SIDE_POINTS * TILE_SIDE_POINTS), 0.3, 1.8, ((0, 16), (1, 2)), jnp.float32),
        "thermal_subcooling": bell_draw(key_list[2], (SHEET_COUNT, TILES_IN_SHEET, TILE_SIDE_POINTS, TILE_SIDE_POINTS * TILE_SIDE_POINTS), 0.3, 1.8, ((0, 16), (1, 2)), jnp.float32),
        "holder_places_prior": draw_holder_places_prior(jax.random.fold_in(key_list[6], 71), 0),
        "holder_places_revised": draw_holder_places_revised(jax.random.fold_in(key_list[6], 71), 0),
        "update_flags": set_ends((jax.random.randint(key_list[5], (SHEET_COUNT, TILES_IN_SHEET), 0, 4) < 3).astype(jnp.int32), jax.random.fold_in(key_list[5], 1), 0, 1),
    }


RATE = 0.1
ANISO = 0.05
COUPLE = 0.5
DIFF_SOLUTE = 0.08
DIFF_HEAT = 0.15
TINY = 1e-4


def laplace(center, neighbours):
    return ((neighbours[0] + neighbours[1]) + (neighbours[2] + neighbours[3])) + (neighbours[4] + neighbours[5]) - 6.0 * center


def march_forward(phase_now, solute_now, heat_now, near_phase, near_solute, near_heat, active_now):
    slope_x = 0.5 * (near_phase[0] - near_phase[1])
    slope_y = 0.5 * (near_phase[2] - near_phase[3])
    slope_z = 0.5 * (near_phase[4] - near_phase[5])
    sq_x = slope_x * slope_x
    sq_y = slope_y * slope_y
    sq_z = slope_z * slope_z
    slope_sq = sq_x + sq_y + sq_z
    quartic = sq_x * sq_x + sq_y * sq_y + sq_z * sq_z
    fourth_ratio = quartic / (slope_sq * slope_sq + TINY)
    anisotropy = (1.0 - 3.0 * ANISO) + 4.0 * ANISO * fourth_ratio
    well_term = 1.0 - phase_now * phase_now
    forcing = phase_now - phase_now * phase_now * phase_now - COUPLE * well_term * well_term * (solute_now + heat_now)
    phase_new = phase_now + active_now * (RATE * (anisotropy * anisotropy * laplace(phase_now, near_phase) + forcing))
    change = phase_new - phase_now
    solute_new = solute_now + DIFF_SOLUTE * laplace(solute_now, near_solute) + 0.5 * change
    heat_new = heat_now + DIFF_HEAT * laplace(heat_now, near_heat) + 0.5 * change
    return phase_new, solute_new, heat_new


def mesh_adjacent(grid):
    x_upper = jnp.concatenate([grid[1:], grid[-1:]], axis=0)
    x_lower = jnp.concatenate([grid[:1], grid[:-1]], axis=0)
    y_upper = jnp.roll(grid, -1, axis=1)
    y_lower = jnp.roll(grid, 1, axis=1)
    z_upper = jnp.roll(grid, -1, axis=2)
    z_lower = jnp.roll(grid, 1, axis=2)
    return (x_upper, x_lower, y_upper, y_lower, z_upper, z_lower)


def arrange_as_mesh(blocks, slots):
    inverse = jnp.argsort(slots, axis=1).astype(jnp.int32)
    placed = jnp.take_along_axis(blocks, inverse[:, :, None, None], axis=1)
    placed = placed.reshape(SHEET_COUNT, BY, BZ, TILE_SIDE_POINTS, TILE_SIDE_POINTS, TILE_SIDE_POINTS)
    return placed.transpose(0, 3, 1, 4, 2, 5).reshape(SHEET_COUNT * TILE_SIDE_POINTS, BY * TILE_SIDE_POINTS, BZ * TILE_SIDE_POINTS)


def unpack_mesh(grid, slots):
    placed = grid.reshape(SHEET_COUNT, TILE_SIDE_POINTS, BY, TILE_SIDE_POINTS, BZ, TILE_SIDE_POINTS).transpose(0, 2, 4, 1, 3, 5)
    placed = placed.reshape(SHEET_COUNT, TILES_IN_SHEET, TILE_SIDE_POINTS, TILE_SIDE_POINTS * TILE_SIDE_POINTS)
    return jnp.take_along_axis(placed, slots.astype(jnp.int32)[:, :, None, None], axis=1)


def reference(order_parameter, concentration_excess, thermal_subcooling, holder_places_prior, holder_places_revised, update_flags):
    order_parameter_mesh = arrange_as_mesh(order_parameter, holder_places_prior)
    concentration_mesh = arrange_as_mesh(concentration_excess, holder_places_prior)
    thermal_mesh = arrange_as_mesh(thermal_subcooling, holder_places_prior)
    update_flags_mesh = update_flags.astype(jnp.float32).reshape(SHEET_COUNT, 1, BY, 1, BZ, 1)
    update_flags_mesh = jnp.broadcast_to(update_flags_mesh, (SHEET_COUNT, TILE_SIDE_POINTS, BY, TILE_SIDE_POINTS, BZ, TILE_SIDE_POINTS)).reshape(SHEET_COUNT * TILE_SIDE_POINTS, BY * TILE_SIDE_POINTS, BZ * TILE_SIDE_POINTS)
    for sweep_index in range(2 * STEPS):
        order_parameter_mesh, concentration_mesh, thermal_mesh = march_forward(order_parameter_mesh, concentration_mesh, thermal_mesh, mesh_adjacent(order_parameter_mesh), mesh_adjacent(concentration_mesh), mesh_adjacent(thermal_mesh), update_flags_mesh)
    return (unpack_mesh(order_parameter_mesh, holder_places_revised), unpack_mesh(concentration_mesh, holder_places_revised), unpack_mesh(thermal_mesh, holder_places_revised))
```

```python
import functools

import jax
import jax.numpy as jnp
from jax import lax
from jax.experimental import pallas as pl
from jax.experimental.pallas import tpu as pltpu
from jax.sharding import PartitionSpec as P

RATE = 0.1
ANISO = 0.05
COUPLE = 0.5
DIFF_SOLUTE = 0.08
DIFF_HEAT = 0.15
TINY = 0.0001
ROWS, LANES = 8, 128
EDGE = 2
FIELDS = 3
AXES = ("slab", "bal")
VMEM_BYTES = 40 * 2**20


def tiles_of(block):
    blocks, side, cells = block.shape
    split = block.reshape(blocks, side // ROWS, ROWS, cells // LANES, LANES)
    return split.transpose(0, 1, 3, 2, 4).reshape(blocks, side * cells // LANES, LANES)


def block_of(tiles, side):
    blocks, rows, _ = tiles.shape
    columns = rows // side
    split = tiles.reshape(blocks, side // ROWS, columns, ROWS, LANES)
    return split.transpose(0, 1, 3, 2, 4).reshape(blocks, side, columns * LANES)


def plane_rows(x):
    return pl.ds((x // ROWS) * ROWS * ROWS + x % ROWS, ROWS, stride=ROWS)


def lane_ids():
    return lax.broadcasted_iota(jnp.int32, (ROWS, LANES), 1)


class Geometry:
    def __init__(self, side):
        lanes = lane_ids()
        self.side = side
        self.y_last = lanes >= LANES - side
        self.y_first = lanes < side
        self.z_first = lanes % side == 0
        self.z_last = lanes % side == side - 1

    def up(self, plane):
        return pltpu.roll(plane, LANES - self.side, 1)

    def down(self, plane):
        return pltpu.roll(plane, self.side, 1)

    def y_pair(self, up, down):
        upper = jnp.where(self.y_last, pltpu.roll(up, ROWS - 1, 0), up)
        lower = jnp.where(self.y_first, pltpu.roll(down, 1, 0), down)
        return upper, lower

    def z_pair(self, plane, next_down, previous_up):
        upper = pltpu.roll(jnp.where(self.z_first, next_down, plane), LANES - 1, 1)
        lower = pltpu.roll(jnp.where(self.z_last, previous_up, plane), 1, 1)
        return upper, lower


def advance(centers, sums, differences, rate):
    phase, solute, heat = centers
    sum_phase, sum_solute, sum_heat = sums
    squares = [d * d for d in differences]
    square = squares[0] + squares[1] + squares[2]
    quartic = squares[0] * squares[0] + squares[1] * squares[1] + squares[2] * squares[2]
    below = square * square + 16.0 * TINY
    anisotropy = (1.0 - 3.0 * ANISO) + 4.0 * ANISO * (quartic / below)
    well = 1.0 - phase * phase
    forcing = well * (phase - COUPLE * well * (solute + heat))
    change = rate * (anisotropy * anisotropy * (sum_phase - 6.0 * phase) + forcing)
    half = 0.5 * change
    return (
        phase + change,
        (1.0 - 6.0 * DIFF_SOLUTE) * solute + (DIFF_SOLUTE * sum_solute + half),
        (1.0 - 6.0 * DIFF_HEAT) * heat + (DIFF_HEAT * sum_heat + half),
    )


def step_plane(geometry, below, center, above, next_down, previous_up, rate):
    sums, differences = [], None
    for f in range(FIELDS):
        y_upper, y_lower = geometry.y_pair(geometry.up(center[f]), geometry.down(center[f]))
        z_upper, z_lower = geometry.z_pair(center[f], next_down[f], previous_up[f])
        sums.append((above[f] + below[f]) + (y_upper + y_lower) + (z_upper + z_lower))
        if f == 0:
            differences = (above[f] - below[f], y_upper - y_lower, z_upper - z_lower)
    return advance(center, sums, differences, rate)


def step_ring(geometry, load_below, load_center, load_above, rates):
    ring = len(rates)
    centers = [load_center(p) for p in range(ring)]
    ups = [[geometry.up(c) for c in center] for center in centers]
    downs = [[geometry.down(c) for c in center] for center in centers]
    return [
        step_plane(
            geometry,
            load_below(p),
            centers[p],
            load_above(p),
            downs[(p + 1) % ring],
            ups[(p - 1) % ring],
            rates[p],
        )
        for p in range(ring)
    ]


def planes_at(ref, p, x):
    return [ref[f, p, x] for f in range(FIELDS)]


def pack_kernel(side, *refs):
    fields, (even_ref, odd_ref), (tiles, sem) = refs[:FIELDS], refs[FIELDS : FIELDS + 2], refs[FIELDS + 2 :]
    blocks = even_ref.shape[1]
    rows = ROWS * ROWS
    last = side * ROWS - rows
    copies = [
        pltpu.make_async_copy(fields[f].at[:, pl.ds(start, rows)], tiles.at[f, end], sem.at[f, end])
        for f in range(FIELDS)
        for end, start in enumerate((0, last))
    ]
    for copy in copies:
        copy.start()
    parity = lax.rem(lax.axis_index("slab"), 2)
    for copy in copies:
        copy.wait()
    for f in range(FIELDS):
        for b in range(blocks):
            for d in range(EDGE):
                for ref, end in ((even_ref, 1 - parity), (odd_ref, parity)):
                    row = jnp.where(end == 0, d, ROWS - 1 - d)
                    ref[f, b, d] = tiles[f, end, b, pl.ds(row, ROWS, stride=ROWS)]


def inner_kernel(side, blocks, cores, *refs):
    own, other = refs[:FIELDS], refs[FIELDS : 2 * FIELDS]
    before, after, flags = refs[2 * FIELDS : 2 * FIELDS + 3]
    outs = refs[2 * FIELDS + 3 : 3 * FIELDS + 3]
    rim_raw, rim_step, rim_out = refs[3 * FIELDS + 3 : 3 * FIELDS + 6]
    tiles, raw, stepped, result, in_sem, out_sem = refs[3 * FIELDS + 6 :]
    ring = blocks * cores
    layer, core = lax.axis_index("slab"), lax.axis_index("bal")
    copies = []
    for c, source in enumerate((own, other)):
        for f in range(FIELDS):
            copies.append(pltpu.make_async_copy(source[f], tiles.at[c, f], in_sem.at[c, f]))
            copies[-1].start()
    geometry = Geometry(side)
    rates = [jnp.where(flags[p, layer] != 0, jnp.float32(RATE), jnp.float32(0.0)) for p in range(ring)]
    for c in range(cores):
        slot = jnp.where(c == 0, core, cores - 1 - core) * blocks
        for f in range(FIELDS):
            copies[c * FIELDS + f].wait()
            for b in range(blocks):
                p = before[slot + b, layer]

                @pl.loop(0, side, unroll=8)
                def _(x, c=c, f=f, b=b, p=p):
                    raw[f, p, x] = tiles[c, f, b, plane_rows(x)]

    @pl.loop(1, side - 1)
    def _(x):
        new = step_ring(
            geometry,
            lambda p: planes_at(raw, p, x - 1),
            lambda p: planes_at(raw, p, x),
            lambda p: planes_at(raw, p, x + 1),
            rates,
        )
        for p in range(ring):
            for f in range(FIELDS):
                stepped[f, p, x] = new[p][f]

    for end in range(2):
        for d in range(EDGE):
            for f in range(FIELDS):
                for p in range(ring):
                    rim_raw[end, f, p, d] = raw[f, p, d if end == 0 else side - 1 - d]
                    rim_step[end, f, p, d] = stepped[f, p, 1 + d if end == 0 else side - 2 - d]

    places = [after[core * blocks + b, layer] for b in range(blocks)]

    @pl.loop(2, side - 2)
    def _(x):
        for b in range(blocks):
            p = places[b]
            following, previous = lax.rem(p + 1, ring), lax.rem(p + ring - 1, ring)
            new = step_plane(
                geometry,
                planes_at(stepped, p, x - 1),
                planes_at(stepped, p, x),
                planes_at(stepped, p, x + 1),
                [geometry.down(c) for c in planes_at(stepped, following, x)],
                [geometry.up(c) for c in planes_at(stepped, previous, x)],
                jnp.where(flags[p, layer] != 0, jnp.float32(RATE), jnp.float32(0.0)),
            )
            for f in range(FIELDS):
                result[f, b, plane_rows(x)] = new[f]

    rows = ROWS * ROWS
    middle = pl.ds(rows, side * ROWS - 2 * rows)
    copies = []
    for f in range(FIELDS):
        copies.append(pltpu.make_async_copy(result.at[f, :, middle], outs[f].at[:, middle], out_sem.at[f]))
        copies[-1].start()
    for f in range(FIELDS):
        for end in range(2):
            part = pl.ds(end * (side * ROWS - rows), rows)
            rim_out[f, end] = result[f, :, part]
    for copy in copies:
        copy.wait()


def rim_kernel(side, blocks, cores, layers, *refs):
    rim_raw, rim_step, rim_out = refs[:3]
    even, odd, even_other, odd_other = refs[3:7]
    before, after, flags = refs[7:10]
    outs = refs[10 + FIELDS : 10 + 2 * FIELDS]
    halo, stepped, tiles, sem = refs[10 + 2 * FIELDS :]
    ring = blocks * cores
    layer, core = lax.axis_index("slab"), lax.axis_index("bal")
    parity = lax.rem(layer, 2)
    geometry = Geometry(side)
    rows = ROWS * ROWS

    def rate_of(which, p):
        return jnp.where(flags[p, which] != 0, jnp.float32(RATE), jnp.float32(0.0))

    for f in range(FIELDS):
        for end in range(2):
            tiles[f, end] = rim_out[f, end]

    for message, pair in enumerate(((even, even_other), (odd, odd_other))):
        end = (1 - parity) if message == 0 else parity
        beside = layer + 2 * end - 1
        outside = jnp.logical_or(beside < 0, beside >= layers)
        table = jnp.clip(beside, 0, layers - 1)

        @pl.when(jnp.logical_not(outside))
        def _(pair=pair, end=end, table=table):
            for c in range(cores):
                slot = jnp.where(c == 0, core, cores - 1 - core) * blocks
                for b in range(blocks):
                    p = before[slot + b, table]
                    for f in range(FIELDS):
                        for d in range(EDGE):
                            halo[end, f, p, d] = pair[c][f, b, d]

        @pl.when(outside)
        def _(end=end):
            for p in range(ring):
                for f in range(FIELDS):
                    for d in range(EDGE):
                        halo[end, f, p, d] = rim_raw[end, f, p, 0]

    def at(ref, end, p, d):
        return [ref[end, f, p, d] for f in range(FIELDS)]

    places = [after[core * blocks + b, layer] for b in range(blocks)]
    copies = []
    for end in range(2):
        beside = layer + 2 * end - 1
        outside = jnp.logical_or(beside < 0, beside >= layers)
        table = jnp.clip(beside, 0, layers - 1)
        face = step_ring(
            geometry,
            lambda p: at(halo, end, p, 0),
            lambda p: at(rim_raw, end, p, 0),
            lambda p: at(rim_raw, end, p, 1),
            [rate_of(layer, p) for p in range(ring)],
        )
        beyond = step_ring(
            geometry,
            lambda p: at(halo, end, p, 1),
            lambda p: at(halo, end, p, 0),
            lambda p: at(rim_raw, end, p, 0),
            [rate_of(table, p) for p in range(ring)],
        )
        for p in range(ring):
            for f in range(FIELDS):
                stepped[end, f, p, 0] = jnp.where(outside, face[p][f], beyond[p][f])
                stepped[end, f, p, 1] = face[p][f]
                for d in range(EDGE):
                    stepped[end, f, p, 2 + d] = rim_step[end, f, p, d]
        for d in range(EDGE):
            for b in range(blocks):
                p = places[b]
                following, previous = lax.rem(p + 1, ring), lax.rem(p + ring - 1, ring)
                new = step_plane(
                    geometry,
                    at(stepped, end, p, d),
                    at(stepped, end, p, d + 1),
                    at(stepped, end, p, d + 2),
                    [geometry.down(c) for c in at(stepped, end, following, d + 1)],
                    [geometry.up(c) for c in at(stepped, end, previous, d + 1)],
                    rate_of(layer, p),
                )
                row = d if end == 0 else ROWS - 1 - d
                for f in range(FIELDS):
                    tiles[f, end, b, pl.ds(row, ROWS, stride=ROWS)] = new[f]
        for f in range(FIELDS):
            part = pl.ds(end * (side * ROWS - rows), rows)
            copies.append(pltpu.make_async_copy(tiles.at[f, end], outs[f].at[:, part], sem.at[f, end]))
            copies[-1].start()
    for copy in copies:
        copy.wait()


def neighbour_swaps(layers, cores, first):
    pairs = []
    for layer in range(layers):
        partner = layer + 1 if (layer - first) % 2 == 0 else layer - 1
        for core in range(cores):
            here = layer * cores + core
            if 0 <= partner < layers:
                pairs.append((here, partner * cores + core))
            else:
                pairs.append((here, layer * cores + cores - 1 - core))
    return pairs


def body(layers, cores, order_parameter, concentration_excess, thermal_subcooling, before, after, flags):
    blocks, side = order_parameter.shape[1], order_parameter.shape[2]
    ring = blocks * cores
    rows = side * ROWS
    f32 = jnp.float32
    before, after, flags = before.T, after.T, flags.T
    owners = [(s * cores + c, s * cores + cores - 1 - c) for s in range(layers) for c in range(cores)]
    fields = [tiles_of(a[0]) for a in (order_parameter, concentration_excess, thermal_subcooling)]
    others = [lax.ppermute(a, AXES, owners) for a in fields]
    vmem, hbm, smem = (pl.BlockSpec(memory_space=m) for m in (pltpu.VMEM, pl.ANY, pltpu.SMEM))
    message = jax.ShapeDtypeStruct((FIELDS, blocks, EDGE, ROWS, LANES), f32)
    even, odd = pl.pallas_call(
        functools.partial(pack_kernel, side),
        out_shape=(message, message),
        in_specs=[hbm] * FIELDS,
        out_specs=(vmem, vmem),
        scratch_shapes=[
            pltpu.VMEM((FIELDS, 2, blocks, ROWS * ROWS, LANES), f32),
            pltpu.SemaphoreType.DMA((FIELDS, 2)),
        ],
        compiler_params=pltpu.CompilerParams(vmem_limit_bytes=VMEM_BYTES),
        cost_estimate=pl.CostEstimate(flops=0, bytes_accessed=10**6, transcendentals=0),
    )(*fields)
    odd_in = lax.ppermute(odd, AXES, neighbour_swaps(layers, cores, 1))
    even_in = lax.ppermute(even, AXES, neighbour_swaps(layers, cores, 0))
    rim = jax.ShapeDtypeStruct((2, FIELDS, ring, EDGE, ROWS, LANES), f32)
    whole = jax.ShapeDtypeStruct((blocks, rows, LANES), f32)
    rim_tiles = (FIELDS, 2, blocks, ROWS * ROWS, LANES)
    *parts, rim_raw, rim_step, rim_out = pl.pallas_call(
        functools.partial(inner_kernel, side, blocks, cores),
        out_shape=(whole,) * FIELDS + (rim, rim, jax.ShapeDtypeStruct(rim_tiles, f32)),
        in_specs=[hbm] * (2 * FIELDS) + [smem] * 3,
        out_specs=(hbm,) * FIELDS + (vmem,) * 3,
        scratch_shapes=[
            pltpu.VMEM((cores, FIELDS, blocks, rows, LANES), f32),
            pltpu.VMEM((FIELDS, ring, side, ROWS, LANES), f32),
            pltpu.VMEM((FIELDS, ring, side, ROWS, LANES), f32),
            pltpu.VMEM((FIELDS, blocks, rows, LANES), f32),
            pltpu.SemaphoreType.DMA((cores, FIELDS)),
            pltpu.SemaphoreType.DMA((FIELDS,)),
        ],
        compiler_params=pltpu.CompilerParams(vmem_limit_bytes=VMEM_BYTES),
        cost_estimate=pl.CostEstimate(flops=0, bytes_accessed=10**7, transcendentals=0),
    )(*fields, *others, before, after, flags)
    odd_in, even_in, rim_raw = lax.optimization_barrier((odd_in, even_in, rim_raw))
    odd_other = lax.ppermute(odd_in, AXES, owners)
    even_other = lax.ppermute(even_in, AXES, owners)
    results = pl.pallas_call(
        functools.partial(rim_kernel, side, blocks, cores, layers),
        out_shape=(whole,) * FIELDS,
        in_specs=[vmem] * 7 + [smem] * 3 + [hbm] * FIELDS,
        out_specs=(hbm,) * FIELDS,
        input_output_aliases={10 + f: f for f in range(FIELDS)},
        scratch_shapes=[
            pltpu.VMEM((2, FIELDS, ring, EDGE, ROWS, LANES), f32),
            pltpu.VMEM((2, FIELDS, ring, 2 + EDGE, ROWS, LANES), f32),
            pltpu.VMEM(rim_tiles, f32),
            pltpu.SemaphoreType.DMA((FIELDS, 2)),
        ],
        compiler_params=pltpu.CompilerParams(vmem_limit_bytes=VMEM_BYTES),
        cost_estimate=pl.CostEstimate(flops=0, bytes_accessed=10**6, transcendentals=0),
    )(rim_raw, rim_step, rim_out, even_in, odd_in, even_other, odd_other, before, after, flags, *parts)
    return tuple(block_of(r, side)[None] for r in results)


def solution(mesh):
    layers, cores = mesh.shape["slab"], mesh.shape["bal"]
    split, copied = P("slab", "bal", None, None), P()
    return jax.shard_map(
        functools.partial(body, layers, cores),
        mesh=mesh,
        in_specs=(split,) * 3 + (copied,) * 3,
        out_specs=(split,) * 3,
        check_vma=False,
    )
```

```python
import functools

import jax
import jax.numpy as jnp
from jax import lax
from jax.experimental import pallas as pl
from jax.experimental.pallas import tpu as pltpu
from jax.sharding import PartitionSpec as P

RATE = 0.1
ANISO = 0.05
COUPLE = 0.5
DIFF_SOLUTE = 0.08
DIFF_HEAT = 0.15
TINY = 0.0001
ROWS, LANES = 8, 128
EDGE = 2
FIELDS = 3
AXES = ("slab", "bal")
UNROLL_FIRST = 6
UNROLL_SECOND = 7
VMEM_BYTES = 40 * 2**20


def tiles_of(block):
    blocks, side, cells = block.shape
    split = block.reshape(blocks, side // ROWS, ROWS, cells // LANES, LANES)
    return split.transpose(0, 1, 3, 2, 4).reshape(blocks, side * cells // LANES, LANES)


def block_of(tiles, side):
    blocks, rows, _ = tiles.shape
    columns = rows // side
    split = tiles.reshape(blocks, side // ROWS, columns, ROWS, LANES)
    return split.transpose(0, 1, 3, 2, 4).reshape(blocks, side, columns * LANES)


def plane_rows(x):
    return pl.ds((x // ROWS) * ROWS * ROWS + x % ROWS, ROWS, stride=ROWS)


def lane_ids():
    return lax.broadcasted_iota(jnp.int32, (ROWS, LANES), 1)


class Geometry:
    def __init__(self, side):
        lanes = lane_ids()
        self.side = side
        self.y_last = lanes >= LANES - side
        self.y_first = lanes < side
        self.z_first = lanes % side == 0
        self.z_last = lanes % side == side - 1

    def up(self, plane):
        return pltpu.roll(plane, LANES - self.side, 1)

    def down(self, plane):
        return pltpu.roll(plane, self.side, 1)

    def y_pair(self, up, down):
        upper = jnp.where(self.y_last, pltpu.roll(up, ROWS - 1, 0), up)
        lower = jnp.where(self.y_first, pltpu.roll(down, 1, 0), down)
        return upper, lower

    def z_pair(self, plane, next_down, previous_up):
        upper = pltpu.roll(jnp.where(self.z_first, next_down, plane), LANES - 1, 1)
        lower = pltpu.roll(jnp.where(self.z_last, previous_up, plane), 1, 1)
        return upper, lower


def advance(centers, sums, differences, rate):
    phase, solute, heat = centers
    sum_phase, sum_solute, sum_heat = sums
    squares = [d * d for d in differences]
    square = squares[0] + squares[1] + squares[2]
    quartic = squares[0] * squares[0] + squares[1] * squares[1] + squares[2] * squares[2]
    below = square * square + 16.0 * TINY
    anisotropy = (1.0 - 3.0 * ANISO) + 4.0 * ANISO * (quartic / below)
    well = 1.0 - phase * phase
    forcing = well * (phase - COUPLE * well * (solute + heat))
    change = rate * (anisotropy * anisotropy * (sum_phase - 6.0 * phase) + forcing)
    half = 0.5 * change
    return (
        phase + change,
        (1.0 - 6.0 * DIFF_SOLUTE) * solute + (DIFF_SOLUTE * sum_solute + half),
        (1.0 - 6.0 * DIFF_HEAT) * heat + (DIFF_HEAT * sum_heat + half),
    )


def step_plane(geometry, below, center, above, up, down, next_down, previous_up, rate):
    sums, differences = [], None
    for f in range(FIELDS):
        y_upper, y_lower = geometry.y_pair(up[f], down[f])
        z_upper, z_lower = geometry.z_pair(center[f], next_down[f], previous_up[f])
        sums.append((above[f] + below[f]) + (y_upper + y_lower) + (z_upper + z_lower))
        if f == 0:
            differences = (above[f] - below[f], y_upper - y_lower, z_upper - z_lower)
    return advance(center, sums, differences, rate)


def step_ring(geometry, load_below, load_center, load_above, rates):
    ring = len(rates)
    centers = [load_center(p) for p in range(ring)]
    ups = [[geometry.up(c) for c in center] for center in centers]
    downs = [[geometry.down(c) for c in center] for center in centers]
    return [
        step_plane(
            geometry,
            load_below(p),
            centers[p],
            load_above(p),
            ups[p],
            downs[p],
            downs[(p + 1) % ring],
            ups[(p - 1) % ring],
            rates[p],
        )
        for p in range(ring)
    ]


def planes_at(ref, p, x):
    return [ref[f, p, x] for f in range(FIELDS)]


def rate_of(active):
    return jnp.where(active != 0, jnp.float32(RATE), jnp.float32(0.0))


def start_tables(tables, held, sem):
    copies = [pltpu.make_async_copy(t, h, sem.at[i]) for i, (t, h) in enumerate(zip(tables, held))]
    for copy in copies:
        copy.start()
    return copies


def holders(before, layer, core, blocks, cores):
    found = [0] * (blocks * cores)
    for place in range(blocks * cores):
        owner = core if place < blocks else cores - 1 - core
        at = before[owner * blocks + place % blocks, layer]
        found = [jnp.where(at == p, place, found[p]) for p in range(len(found))]
    return found


def pack_kernel(side, *refs):
    fields, (even_ref, odd_ref), (tiles, sem) = refs[:FIELDS], refs[FIELDS : FIELDS + 2], refs[FIELDS + 2 :]
    blocks = even_ref.shape[1]
    rows = ROWS * ROWS
    last = side * ROWS - rows
    copies = [
        pltpu.make_async_copy(fields[f].at[:, pl.ds(start, rows)], tiles.at[f, end], sem.at[f, end])
        for f in range(FIELDS)
        for end, start in enumerate((0, last))
    ]
    for copy in copies:
        copy.start()
    parity = lax.rem(lax.axis_index("slab"), 2)
    for copy in copies:
        copy.wait()
    for f in range(FIELDS):
        for b in range(blocks):
            for d in range(EDGE):
                for ref, end in ((even_ref, 1 - parity), (odd_ref, parity)):
                    row = jnp.where(end == 0, d, ROWS - 1 - d)
                    ref[f, b, d] = tiles[f, end, b, pl.ds(row, ROWS, stride=ROWS)]


def first_kernel(side, blocks, cores, *refs):
    own, other, tables = refs[:FIELDS], refs[FIELDS : 2 * FIELDS], refs[2 * FIELDS : 2 * FIELDS + 2]
    raw, stepped = refs[2 * FIELDS + 2 : 2 * FIELDS + 4]
    tiles, ups, downs, before, flags, sem, own_sem = refs[2 * FIELDS + 4 :]
    ring = blocks * cores
    layer, core = lax.axis_index("slab"), lax.axis_index("bal")
    own_copies = [pltpu.make_async_copy(own[f], tiles.at[f], own_sem.at[f]) for f in range(FIELDS)]
    for copy in own_copies:
        copy.start()
    copies = start_tables(tables, (before, flags), sem)
    geometry = Geometry(side)
    for c, source in ((1, other), (0, [tiles.at[f] for f in range(FIELDS)])):
        for f in range(FIELDS):
            if c == 0:
                own_copies[f].wait()
            for b in range(blocks):
                for x in range(side):
                    plane = source[f][b, plane_rows(x)]
                    raw[f, c * blocks + b, x] = plane
                    ups[f, c * blocks + b, x] = geometry.up(plane)
                    downs[f, c * blocks + b, x] = geometry.down(plane)
    for copy in copies:
        copy.wait()
    places = holders(before, layer, core, blocks, cores)
    rates = [rate_of(flags[p, layer]) for p in range(ring)]

    @pl.loop(1, side - 1, unroll=UNROLL_FIRST)
    def _(x):
        for p in range(ring):
            here, following, previous = places[p], places[(p + 1) % ring], places[(p - 1) % ring]
            new = step_plane(
                geometry,
                planes_at(raw, here, x - 1),
                planes_at(raw, here, x),
                planes_at(raw, here, x + 1),
                planes_at(ups, here, x),
                planes_at(downs, here, x),
                planes_at(downs, following, x),
                planes_at(ups, previous, x),
                rates[p],
            )
            for f in range(FIELDS):
                stepped[f, p, x] = new[f]


def second_kernel(side, blocks, cores, *refs):
    stepped, tables, outs, rim_out = refs[0], refs[1:3], refs[3 : 3 + FIELDS], refs[3 + FIELDS]
    result, after, flags, sem, out_sem = refs[4 + FIELDS :]
    ring = blocks * cores
    layer, core = lax.axis_index("slab"), lax.axis_index("bal")
    copies = start_tables(tables, (after, flags), sem)
    geometry = Geometry(side)
    for copy in copies:
        copy.wait()
    places = [after[core * blocks + b, layer] for b in range(blocks)]
    rates = [rate_of(flags[p, layer]) for p in places]
    rows = ROWS * ROWS

    @pl.loop(2, side - 2, unroll=UNROLL_SECOND)
    def _(x):
        for b in range(blocks):
            p = places[b]
            following, previous = lax.rem(p + 1, ring), lax.rem(p + ring - 1, ring)
            center = planes_at(stepped, p, x)
            new = step_plane(
                geometry,
                planes_at(stepped, p, x - 1),
                center,
                planes_at(stepped, p, x + 1),
                [geometry.up(c) for c in center],
                [geometry.down(c) for c in center],
                [geometry.down(c) for c in planes_at(stepped, following, x)],
                [geometry.up(c) for c in planes_at(stepped, previous, x)],
                rates[b],
            )
            for f in range(FIELDS):
                result[f, b, plane_rows(x)] = new[f]

    middle = pl.ds(rows, side * ROWS - 2 * rows)
    copies = []
    for f in range(FIELDS):
        copies.append(pltpu.make_async_copy(result.at[f, :, middle], outs[f].at[:, middle], out_sem.at[f]))
        copies[-1].start()
    for f in range(FIELDS):
        for end in range(2):
            part = pl.ds(end * (side * ROWS - rows), rows)
            rim_out[f, end] = result[f, :, part]
    for copy in copies:
        copy.wait()


def rim_kernel(side, blocks, cores, layers, *refs):
    raw, inner, rim_out = refs[:3]
    even, odd, even_other, odd_other = refs[3:7]
    tables = refs[7:10]
    outs = refs[10 + FIELDS : 10 + 2 * FIELDS]
    halo, stepped, tiles, before, after, flags, table_sem, sem = refs[10 + 2 * FIELDS :]
    ring = blocks * cores
    layer, core = lax.axis_index("slab"), lax.axis_index("bal")
    parity = lax.rem(layer, 2)
    table_copies = start_tables(tables, (before, after, flags), table_sem)
    geometry = Geometry(side)
    rows = ROWS * ROWS
    for f in range(FIELDS):
        for end in range(2):
            tiles[f, end] = rim_out[f, end]
    for copy in table_copies:
        copy.wait()
    places = holders(before, layer, core, blocks, cores)

    def at_raw(end, p, d):
        return planes_at(raw, places[p], d if end == 0 else side - 1 - d)

    for message, pair in enumerate(((even, even_other), (odd, odd_other))):
        end = (1 - parity) if message == 0 else parity
        beside = layer + 2 * end - 1
        outside = jnp.logical_or(beside < 0, beside >= layers)
        table = jnp.clip(beside, 0, layers - 1)

        @pl.when(jnp.logical_not(outside))
        def _(pair=pair, end=end, table=table):
            for c in range(cores):
                slot = jnp.where(c == 0, core, cores - 1 - core) * blocks
                for b in range(blocks):
                    p = before[slot + b, table]
                    for f in range(FIELDS):
                        for d in range(EDGE):
                            halo[end, f, p, d] = pair[c][f, b, d]

        @pl.when(outside)
        def _(end=end):
            x = end * (side - 1)
            for p in range(ring):
                for f in range(FIELDS):
                    for d in range(EDGE):
                        halo[end, f, p, d] = raw[f, places[p], x]

    def at(ref, end, p, d):
        return [ref[end, f, p, d] for f in range(FIELDS)]

    copies = []
    for end in range(2):
        beside = layer + 2 * end - 1
        outside = jnp.logical_or(beside < 0, beside >= layers)
        table = jnp.clip(beside, 0, layers - 1)
        face = step_ring(
            geometry,
            lambda p: at(halo, end, p, 0),
            lambda p: at_raw(end, p, 0),
            lambda p: at_raw(end, p, 1),
            [rate_of(flags[p, layer]) for p in range(ring)],
        )
        beyond = step_ring(
            geometry,
            lambda p: at(halo, end, p, 1),
            lambda p: at(halo, end, p, 0),
            lambda p: at_raw(end, p, 0),
            [rate_of(flags[p, table]) for p in range(ring)],
        )
        for p in range(ring):
            for f in range(FIELDS):
                stepped[end, f, p, 0] = jnp.where(outside, face[p][f], beyond[p][f])
                stepped[end, f, p, 1] = face[p][f]
                for d in range(EDGE):
                    stepped[end, f, p, 2 + d] = inner[f, p, 1 + d if end == 0 else side - 2 - d]
    for end in range(2):
        for d in range(EDGE):
            for b in range(blocks):
                p = after[core * blocks + b, layer]
                following, previous = lax.rem(p + 1, ring), lax.rem(p + ring - 1, ring)
                center = at(stepped, end, p, d + 1)
                new = step_plane(
                    geometry,
                    at(stepped, end, p, d),
                    center,
                    at(stepped, end, p, d + 2),
                    [geometry.up(c) for c in center],
                    [geometry.down(c) for c in center],
                    [geometry.down(c) for c in at(stepped, end, following, d + 1)],
                    [geometry.up(c) for c in at(stepped, end, previous, d + 1)],
                    rate_of(flags[p, layer]),
                )
                row = d if end == 0 else ROWS - 1 - d
                for f in range(FIELDS):
                    tiles[f, end, b, pl.ds(row, ROWS, stride=ROWS)] = new[f]
        for f in range(FIELDS):
            part = pl.ds(end * (side * ROWS - rows), rows)
            copies.append(pltpu.make_async_copy(tiles.at[f, end], outs[f].at[:, part], sem.at[f, end]))
            copies[-1].start()
    for copy in copies:
        copy.wait()


def neighbour_swaps(layers, cores, first):
    pairs = []
    for layer in range(layers):
        partner = layer + 1 if (layer - first) % 2 == 0 else layer - 1
        for core in range(cores):
            here = layer * cores + core
            if 0 <= partner < layers:
                pairs.append((here, partner * cores + core))
            else:
                pairs.append((here, layer * cores + cores - 1 - core))
    return pairs


def body(layers, cores, order_parameter, concentration_excess, thermal_subcooling, before, after, flags):
    blocks, side = order_parameter.shape[1], order_parameter.shape[2]
    ring = blocks * cores
    rows = side * ROWS
    f32 = jnp.float32
    before, after, flags = before.T, after.T, flags.T
    owners = [(s * cores + c, s * cores + cores - 1 - c) for s in range(layers) for c in range(cores)]
    fields = [tiles_of(a[0]) for a in (order_parameter, concentration_excess, thermal_subcooling)]
    others = [lax.ppermute(a, AXES, owners) for a in fields]
    vmem, hbm = (pl.BlockSpec(memory_space=m) for m in (pltpu.VMEM, pltpu.HBM))
    params = pltpu.CompilerParams(vmem_limit_bytes=VMEM_BYTES)
    message = jax.ShapeDtypeStruct((FIELDS, blocks, EDGE, ROWS, LANES), f32)
    table = pltpu.SMEM(before.shape, jnp.int32)
    in_hbm = lambda *arrays: [pltpu.with_memory_space_constraint(a, pltpu.HBM) for a in arrays]
    even, odd = pl.pallas_call(
        functools.partial(pack_kernel, side),
        out_shape=(message, message),
        in_specs=[hbm] * FIELDS,
        out_specs=(vmem, vmem),
        scratch_shapes=[
            pltpu.VMEM((FIELDS, 2, blocks, ROWS * ROWS, LANES), f32),
            pltpu.SemaphoreType.DMA((FIELDS, 2)),
        ],
        compiler_params=params,
        cost_estimate=pl.CostEstimate(flops=0, bytes_accessed=10**6, transcendentals=0),
    )(*in_hbm(*fields))
    odd_in = lax.ppermute(odd, AXES, neighbour_swaps(layers, cores, 1))
    even_in = lax.ppermute(even, AXES, neighbour_swaps(layers, cores, 0))
    planes = (FIELDS, ring, side, ROWS, LANES)
    raw, stepped = pl.pallas_call(
        functools.partial(first_kernel, side, blocks, cores),
        out_shape=(jax.ShapeDtypeStruct(planes, f32),) * 2,
        in_specs=[hbm] * FIELDS + [vmem] * FIELDS + [hbm] * 2,
        out_specs=(vmem, vmem),
        scratch_shapes=[pltpu.VMEM((FIELDS, blocks, rows, LANES), f32)]
        + [pltpu.VMEM(planes, f32)] * 2
        + [table] * 2
        + [pltpu.SemaphoreType.DMA((2,)), pltpu.SemaphoreType.DMA((FIELDS,))],
        compiler_params=params,
        cost_estimate=pl.CostEstimate(flops=0, bytes_accessed=10**7, transcendentals=0),
    )(*in_hbm(*fields), *others, *in_hbm(before, flags))
    odd_in, even_in, stepped = lax.optimization_barrier((odd_in, even_in, stepped))
    odd_other = lax.ppermute(odd_in, AXES, owners)
    even_other = lax.ppermute(even_in, AXES, owners)
    whole = jax.ShapeDtypeStruct((blocks, rows, LANES), f32)
    rim_tiles = (FIELDS, 2, blocks, ROWS * ROWS, LANES)
    *parts, rim_out = pl.pallas_call(
        functools.partial(second_kernel, side, blocks, cores),
        out_shape=(whole,) * FIELDS + (jax.ShapeDtypeStruct(rim_tiles, f32),),
        in_specs=[vmem] + [hbm] * 2,
        out_specs=(hbm,) * FIELDS + (vmem,),
        scratch_shapes=[pltpu.VMEM((FIELDS, blocks, rows, LANES), f32)]
        + [table] * 2
        + [pltpu.SemaphoreType.DMA((2,)), pltpu.SemaphoreType.DMA((FIELDS,))],
        compiler_params=params,
        cost_estimate=pl.CostEstimate(flops=0, bytes_accessed=10**7, transcendentals=0),
    )(stepped, *in_hbm(after, flags))
    results = pl.pallas_call(
        functools.partial(rim_kernel, side, blocks, cores, layers),
        out_shape=(whole,) * FIELDS,
        in_specs=[vmem] * 7 + [hbm] * 3 + [hbm] * FIELDS,
        out_specs=(hbm,) * FIELDS,
        input_output_aliases={10 + f: f for f in range(FIELDS)},
        scratch_shapes=[
            pltpu.VMEM((2, FIELDS, ring, EDGE, ROWS, LANES), f32),
            pltpu.VMEM((2, FIELDS, ring, 2 + EDGE, ROWS, LANES), f32),
            pltpu.VMEM(rim_tiles, f32),
        ]
        + [table] * 3
        + [pltpu.SemaphoreType.DMA((3,)), pltpu.SemaphoreType.DMA((FIELDS, 2))],
        compiler_params=params,
        cost_estimate=pl.CostEstimate(flops=0, bytes_accessed=10**6, transcendentals=0),
    )(raw, stepped, rim_out, even_in, odd_in, even_other, odd_other, *in_hbm(before, after, flags, *parts))
    return tuple(block_of(r, side)[None] for r in results)


def solution(mesh):
    layers, cores = mesh.shape["slab"], mesh.shape["bal"]
    split, copied = P("slab", "bal", None, None), P()
    return jax.shard_map(
        functools.partial(body, layers, cores),
        mesh=mesh,
        in_specs=(split,) * 3 + (copied,) * 3,
        out_specs=(split,) * 3,
        check_vma=False,
    )
```

```python
import functools

import jax
import jax.numpy as jnp
from jax import lax
from jax.experimental import pallas as pl
from jax.experimental.pallas import tpu as pltpu
from jax.sharding import PartitionSpec as P

RATE = 0.1
ANISO = 0.05
COUPLE = 0.5
DIFF_SOLUTE = 0.08
DIFF_HEAT = 0.15
TINY = 0.0001
ROWS, LANES = 8, 128
EDGE = 2
FIELDS = 3
AXES = ("slab", "bal")
SPREAD = 32
CHUNK_FIRST = 15
CHUNK_SECOND = 28
VMEM_BYTES = 40 * 2**20


def tiles_of(block):
    blocks, side, cells = block.shape
    split = block.reshape(blocks, side // ROWS, ROWS, cells // LANES, LANES)
    return split.transpose(0, 1, 3, 2, 4).reshape(blocks, side * cells // LANES, LANES)


def block_of(tiles, side):
    blocks, rows, _ = tiles.shape
    columns = rows // side
    split = tiles.reshape(blocks, side // ROWS, columns, ROWS, LANES)
    return split.transpose(0, 1, 3, 2, 4).reshape(blocks, side, columns * LANES)


def plane_rows(x):
    return pl.ds((x >> 3) * ROWS * ROWS + (x & (ROWS - 1)), ROWS, stride=ROWS)


def lane_ids():
    return lax.broadcasted_iota(jnp.int32, (ROWS, LANES), 1)


class Geometry:
    def __init__(self, side):
        lanes = lane_ids()
        self.side = side
        self.y_last = lanes >= LANES - side
        self.y_first = lanes < side
        self.z_first = lanes % side == 0
        self.z_last = lanes % side == side - 1

    def up(self, plane):
        return pltpu.roll(plane, LANES - self.side, 1)

    def down(self, plane):
        return pltpu.roll(plane, self.side, 1)

    def y_pair(self, up, down):
        upper = jnp.where(self.y_last, pltpu.roll(up, ROWS - 1, 0), up)
        lower = jnp.where(self.y_first, pltpu.roll(down, 1, 0), down)
        return upper, lower

    def z_pair(self, plane, next_down, previous_up):
        upper = pltpu.roll(jnp.where(self.z_first, next_down, plane), LANES - 1, 1)
        lower = pltpu.roll(jnp.where(self.z_last, previous_up, plane), 1, 1)
        return upper, lower


def advance(centers, sums, differences, rate):
    phase, solute, heat = centers
    sum_phase, sum_solute, sum_heat = sums
    squares = [d * d for d in differences]
    square = squares[0] + squares[1] + squares[2]
    quartic = squares[0] * squares[0] + squares[1] * squares[1] + squares[2] * squares[2]
    below = square * square + 16.0 * TINY
    anisotropy = (1.0 - 3.0 * ANISO) + 4.0 * ANISO * (quartic / below)
    well = 1.0 - phase * phase
    forcing = well * (phase - COUPLE * well * (solute + heat))
    change = rate * (anisotropy * anisotropy * (sum_phase - 6.0 * phase) + forcing)
    half = 0.5 * change
    return (
        phase + change,
        (1.0 - 6.0 * DIFF_SOLUTE) * solute + (DIFF_SOLUTE * sum_solute + half),
        (1.0 - 6.0 * DIFF_HEAT) * heat + (DIFF_HEAT * sum_heat + half),
    )


def sides(geometry, center, up, down, next_down, previous_up, phase):
    y_upper, y_lower = geometry.y_pair(up, down)
    z_upper, z_lower = geometry.z_pair(center, next_down, previous_up)
    total = (y_upper + y_lower) + (z_upper + z_lower)
    return (total, y_upper - y_lower, z_upper - z_lower) if phase else (total,)


def keep_sides(geometry, around, b, x, center, up, down, next_down, previous_up):
    for f in range(FIELDS):
        found = sides(geometry, center(f), up(f), down(f), next_down(f), previous_up(f), f == 0)
        for k, value in enumerate(found):
            around[f if k == 0 else FIELDS - 1 + k, b, x] = value


def finish(below, center, above, around, rate):
    sums = [(above[f] + below[f]) + around[f] for f in range(FIELDS)]
    return advance(center, sums, (above[0] - below[0], around[FIELDS], around[FIELDS + 1]), rate)


def step_plane(geometry, below, center, above, up, down, next_down, previous_up, rate):
    around = [
        sides(geometry, center[f], up[f], down[f], next_down[f], previous_up[f], f == 0) for f in range(FIELDS)
    ]
    return finish(below, center, above, [a[0] for a in around] + list(around[0][1:]), rate)


def step_ring(geometry, load_below, load_center, load_above, rates):
    ring = len(rates)
    centers = [load_center(p) for p in range(ring)]
    ups = [[geometry.up(c) for c in center] for center in centers]
    downs = [[geometry.down(c) for c in center] for center in centers]
    return [
        step_plane(
            geometry,
            load_below(p),
            centers[p],
            load_above(p),
            ups[p],
            downs[p],
            downs[(p + 1) % ring],
            ups[(p - 1) % ring],
            rates[p],
        )
        for p in range(ring)
    ]


def planes_at(ref, p, x):
    return [ref[f, p, x] for f in range(FIELDS)]


def rate_of(active):
    return jnp.where(active != 0, jnp.float32(RATE), jnp.float32(0.0))


def start_tables(tables, held, sem):
    copies = [pltpu.make_async_copy(t, h, sem.at[i]) for i, (t, h) in enumerate(zip(tables, held))]
    for copy in copies:
        copy.start()
    return copies


def holders(before, layer, core, blocks, cores):
    found = [0] * (blocks * cores)
    for place in range(blocks * cores):
        owner = core if place < blocks else cores - 1 - core
        at = before[owner * blocks + place % blocks, layer]
        found = [jnp.where(at == p, place, found[p]) for p in range(len(found))]
    return found


def pack_kernel(side, *refs):
    fields, (even_ref, odd_ref), (tiles, sem) = refs[:FIELDS], refs[FIELDS : FIELDS + 2], refs[FIELDS + 2 :]
    blocks = even_ref.shape[1]
    rows = ROWS * ROWS
    last = side * ROWS - rows
    copies = [
        pltpu.make_async_copy(fields[f].at[:, pl.ds(start, rows)], tiles.at[f, end], sem.at[f, end])
        for f in range(FIELDS)
        for end, start in enumerate((0, last))
    ]
    for copy in copies:
        copy.start()
    parity = lax.rem(lax.axis_index("slab"), 2)
    for copy in copies:
        copy.wait()
    for f in range(FIELDS):
        for b in range(blocks):
            for d in range(EDGE):
                for ref, end in ((even_ref, 1 - parity), (odd_ref, parity)):
                    row = jnp.where(end == 0, d, ROWS - 1 - d)
                    ref[f, b, d] = tiles[f, end, b, pl.ds(row, ROWS, stride=ROWS)]


def first_kernel(side, blocks, cores, layers, *refs):
    own, other, tables = refs[:FIELDS], refs[FIELDS : 2 * FIELDS], refs[2 * FIELDS : 2 * FIELDS + 3]
    raw, stepped, places_out, rates_out = refs[2 * FIELDS + 3 : 2 * FIELDS + 7]
    tiles, ups, downs, around, before, after, flags, sem, own_sem = refs[2 * FIELDS + 7 :]
    ring = blocks * cores
    layer, core = lax.axis_index("slab"), lax.axis_index("bal")
    own_copies = [pltpu.make_async_copy(own[f], tiles.at[f], own_sem.at[f]) for f in range(FIELDS)]
    for copy in own_copies:
        copy.start()
    copies = start_tables(tables, (before, after, flags), sem)
    geometry = Geometry(side)
    def spread(c, f, source):
        @pl.loop(0, side // SPREAD)
        def _(r):
            for s in range(SPREAD):
                x = r * SPREAD + s
                for b in range(blocks):
                    plane = source[b, plane_rows(x)]
                    raw[f, c * blocks + b, x] = plane
                    ups[f, c * blocks + b, x] = geometry.up(plane)
                    downs[f, c * blocks + b, x] = geometry.down(plane)

    for f in range(FIELDS):
        spread(1, f, other[f])
    for f in range(FIELDS):
        own_copies[f].wait()
        spread(0, f, tiles.at[f])
    for copy in copies:
        copy.wait()
    places = holders(before, layer, core, blocks, cores)
    rates = [rate_of(flags[p, layer]) for p in range(ring)]

    @pl.loop(0, (side - 2) // CHUNK_FIRST)
    def _(i):
        for x in [1 + i * CHUNK_FIRST + u for u in range(CHUNK_FIRST)]:
            for p in range(ring):
                here, following, previous = places[p], places[(p + 1) % ring], places[(p - 1) % ring]
                keep_sides(
                    geometry,
                    around,
                    p,
                    x,
                    lambda f: raw[f, here, x],
                    lambda f: ups[f, here, x],
                    lambda f: downs[f, here, x],
                    lambda f: downs[f, following, x],
                    lambda f: ups[f, previous, x],
                )
        for x in [1 + i * CHUNK_FIRST + u for u in range(CHUNK_FIRST)]:
            for p in range(ring):
                low, center, high = (planes_at(raw, places[p], x + d) for d in (-1, 0, 1))
                new = finish(low, center, high, [around[k, p, x] for k in range(FIELDS + 2)], rates[p])
                for f in range(FIELDS):
                    stepped[f, p, x] = new[f]

    beside = [jnp.clip(layer + 2 * end - 1, 0, layers - 1) for end in range(2)]
    listed = places + [after[core * blocks + b, layer] for b in range(blocks)]
    for table in beside:
        for c in range(cores):
            slot = jnp.where(c == 0, core, cores - 1 - core) * blocks
            listed += [before[slot + b, table] for b in range(blocks)]
    for k, place in enumerate(listed):
        places_out[k] = jnp.full((ROWS, LANES), place, jnp.int32)
    rates += [rate_of(flags[p, table]) for table in beside for p in range(ring)]
    for k, rate in enumerate(rates):
        rates_out[k] = jnp.full((ROWS, LANES), rate, jnp.float32)


def place_at(ref, k):
    return ref[k][0, 0]


def second_kernel(side, blocks, cores, *refs):
    stepped, places_ref, rates_ref, result, shifted, around = refs
    ring = blocks * cores
    geometry = Geometry(side)
    places = [place_at(places_ref, ring + b) for b in range(blocks)]
    rates = [rates_ref[p] for p in places]

    @pl.loop(0, (side - 4) // CHUNK_SECOND)
    def _(i):
        planes = [2 + i * CHUNK_SECOND + u for u in range(CHUNK_SECOND)]
        for x in planes:
            for b, p in enumerate(places):
                following, previous = (p + 1) & (ring - 1), (p + ring - 1) & (ring - 1)
                for f in range(FIELDS):
                    shifted[0, f, b, x] = geometry.up(stepped[f, p, x])
                    shifted[1, f, b, x] = geometry.down(stepped[f, p, x])
                    shifted[2, f, b, x] = geometry.down(stepped[f, following, x])
                    shifted[3, f, b, x] = geometry.up(stepped[f, previous, x])
        for x in planes:
            for b, p in enumerate(places):
                keep_sides(
                    geometry,
                    around,
                    b,
                    x,
                    lambda f: stepped[f, p, x],
                    lambda f: shifted[0, f, b, x],
                    lambda f: shifted[1, f, b, x],
                    lambda f: shifted[2, f, b, x],
                    lambda f: shifted[3, f, b, x],
                )
        for x in planes:
            for b, p in enumerate(places):
                low, center, high = (planes_at(stepped, p, x + d) for d in (-1, 0, 1))
                new = finish(low, center, high, [around[k, b, x] for k in range(FIELDS + 2)], rates[b])
                for f in range(FIELDS):
                    result[f, b, plane_rows(x)] = new[f]


def rim_kernel(side, blocks, cores, layers, *refs):
    raw, inner, result, places_ref, rates_ref = refs[:5]
    messages = refs[5:9]
    outs = refs[9 : 9 + FIELDS]
    halo, stepped, tiles, sem, middle_sem = refs[9 + FIELDS :]
    ring = blocks * cores
    layer = lax.axis_index("slab")
    parity = lax.rem(layer, 2)
    geometry = Geometry(side)
    rows = ROWS * ROWS
    middle = pl.ds(rows, side * ROWS - 2 * rows)
    copies = [
        pltpu.make_async_copy(result.at[f, :, middle], outs[f].at[:, middle], middle_sem.at[f])
        for f in range(FIELDS)
    ]
    for copy in copies:
        copy.start()
    places = [place_at(places_ref, p) for p in range(ring)]
    targets = [place_at(places_ref, ring + b) for b in range(blocks)]
    for end in range(2):
        from_even = parity == 1 - end
        for c in range(cores):
            for b in range(blocks):
                p = place_at(places_ref, ring + blocks + (end * cores + c) * blocks + b)
                for f in range(FIELDS):
                    for d in range(EDGE):
                        halo[end, f, p, d] = jnp.where(
                            from_even, messages[2 * c][f, b, d], messages[2 * c + 1][f, b, d]
                        )

    def at(ref, end, p, d):
        return [ref[end, f, p, d] for f in range(FIELDS)]

    for end in range(2):
        beside = layer + 2 * end - 1
        outside = jnp.logical_or(beside < 0, beside >= layers)
        raw_face = [planes_at(raw, places[p], end * (side - 1)) for p in range(ring)]
        raw_next = [planes_at(raw, places[p], 1 + end * (side - 3)) for p in range(ring)]
        near = [
            [jnp.where(outside, r, h) for r, h in zip(raw_face[p], at(halo, end, p, 0))]
            for p in range(ring)
        ]
        face = step_ring(
            geometry,
            lambda p: near[p],
            lambda p: raw_face[p],
            lambda p: raw_next[p],
            [rates_ref[p] for p in range(ring)],
        )
        beyond = step_ring(
            geometry,
            lambda p: at(halo, end, p, 1),
            lambda p: near[p],
            lambda p: raw_face[p],
            [rates_ref[ring * (1 + end) + p] for p in range(ring)],
        )
        for p in range(ring):
            for f in range(FIELDS):
                stepped[end, f, p, 0] = jnp.where(outside, face[p][f], beyond[p][f])
                stepped[end, f, p, 1] = face[p][f]
                for d in range(EDGE):
                    stepped[end, f, p, 2 + d] = inner[f, p, 1 + d if end == 0 else side - 2 - d]
    for f in range(FIELDS):
        for end in range(2):
            tiles[f, end] = result[f, :, pl.ds(end * (side * ROWS - rows), rows)]
    for end in range(2):
        for d in range(EDGE):
            for b in range(blocks):
                p = targets[b]
                following, previous = lax.rem(p + 1, ring), lax.rem(p + ring - 1, ring)
                center = at(stepped, end, p, d + 1)
                new = step_plane(
                    geometry,
                    at(stepped, end, p, d),
                    center,
                    at(stepped, end, p, d + 2),
                    [geometry.up(c) for c in center],
                    [geometry.down(c) for c in center],
                    [geometry.down(c) for c in at(stepped, end, following, d + 1)],
                    [geometry.up(c) for c in at(stepped, end, previous, d + 1)],
                    rates_ref[p],
                )
                row = d if end == 0 else ROWS - 1 - d
                for f in range(FIELDS):
                    tiles[f, end, b, pl.ds(row, ROWS, stride=ROWS)] = new[f]
    for end in range(2):
        for f in range(FIELDS):
            part = pl.ds(end * (side * ROWS - rows), rows)
            copies.append(pltpu.make_async_copy(tiles.at[f, end], outs[f].at[:, part], sem.at[f, end]))
            copies[-1].start()
    for copy in copies:
        copy.wait()


def neighbour_swaps(layers, cores, first):
    pairs = []
    for layer in range(layers):
        partner = layer + 1 if (layer - first) % 2 == 0 else layer - 1
        for core in range(cores):
            here = layer * cores + core
            if 0 <= partner < layers:
                pairs.append((here, partner * cores + core))
            else:
                pairs.append((here, layer * cores + cores - 1 - core))
    return pairs


def body(layers, cores, order_parameter, concentration_excess, thermal_subcooling, before, after, flags):
    blocks, side = order_parameter.shape[1], order_parameter.shape[2]
    ring = blocks * cores
    rows = side * ROWS
    f32 = jnp.float32
    before, after, flags = before.T, after.T, flags.T
    owners = [(s * cores + c, s * cores + cores - 1 - c) for s in range(layers) for c in range(cores)]
    fields = [tiles_of(a[0]) for a in (order_parameter, concentration_excess, thermal_subcooling)]
    others = [lax.ppermute(a, AXES, owners) for a in fields]
    vmem, hbm = (pl.BlockSpec(memory_space=m) for m in (pltpu.VMEM, pltpu.HBM))
    params = pltpu.CompilerParams(vmem_limit_bytes=VMEM_BYTES)
    message = jax.ShapeDtypeStruct((FIELDS, blocks, EDGE, ROWS, LANES), f32)
    table = pltpu.SMEM(before.shape, jnp.int32)
    in_hbm = lambda *arrays: [pltpu.with_memory_space_constraint(a, pltpu.HBM) for a in arrays]
    even, odd = pl.pallas_call(
        functools.partial(pack_kernel, side),
        out_shape=(message, message),
        in_specs=[hbm] * FIELDS,
        out_specs=(vmem, vmem),
        scratch_shapes=[
            pltpu.VMEM((FIELDS, 2, blocks, ROWS * ROWS, LANES), f32),
            pltpu.SemaphoreType.DMA((FIELDS, 2)),
        ],
        compiler_params=params,
        cost_estimate=pl.CostEstimate(flops=0, bytes_accessed=10**6, transcendentals=0),
    )(*in_hbm(*fields))
    odd_in = lax.ppermute(odd, AXES, neighbour_swaps(layers, cores, 1))
    even_in = lax.ppermute(even, AXES, neighbour_swaps(layers, cores, 0))
    planes = (FIELDS, ring, side, ROWS, LANES)
    raw, stepped, places, rates = pl.pallas_call(
        functools.partial(first_kernel, side, blocks, cores, layers),
        out_shape=(
            jax.ShapeDtypeStruct(planes, f32),
            jax.ShapeDtypeStruct(planes, f32),
            jax.ShapeDtypeStruct((3 * ring + blocks, ROWS, LANES), jnp.int32),
            jax.ShapeDtypeStruct((3 * ring, ROWS, LANES), f32),
        ),
        in_specs=[hbm] * FIELDS + [vmem] * FIELDS + [hbm] * 3,
        out_specs=(vmem,) * 4,
        scratch_shapes=[pltpu.VMEM((FIELDS, blocks, rows, LANES), f32)]
        + [pltpu.VMEM(planes, f32)] * 2
        + [pltpu.VMEM((FIELDS + 2, ring, side, ROWS, LANES), f32)]
        + [table] * 3
        + [pltpu.SemaphoreType.DMA((3,)), pltpu.SemaphoreType.DMA((FIELDS,))],
        compiler_params=params,
        cost_estimate=pl.CostEstimate(flops=0, bytes_accessed=10**7, transcendentals=0),
    )(*in_hbm(*fields), *others, *in_hbm(before, after, flags))
    odd_in, even_in, stepped = lax.optimization_barrier((odd_in, even_in, stepped))
    odd_other = lax.ppermute(odd_in, AXES, owners)
    even_other = lax.ppermute(even_in, AXES, owners)
    result = pl.pallas_call(
        functools.partial(second_kernel, side, blocks, cores),
        out_shape=jax.ShapeDtypeStruct((FIELDS, blocks, rows, LANES), f32),
        in_specs=[vmem] * 3,
        out_specs=vmem,
        scratch_shapes=[
            pltpu.VMEM((4, FIELDS, blocks, side, ROWS, LANES), f32),
            pltpu.VMEM((FIELDS + 2, blocks, side, ROWS, LANES), f32),
        ],
        compiler_params=params,
        cost_estimate=pl.CostEstimate(flops=0, bytes_accessed=10**7, transcendentals=0),
    )(stepped, places, rates)
    results = pl.pallas_call(
        functools.partial(rim_kernel, side, blocks, cores, layers),
        out_shape=(jax.ShapeDtypeStruct((blocks, rows, LANES), f32),) * FIELDS,
        in_specs=[vmem] * 9,
        out_specs=(hbm,) * FIELDS,
        scratch_shapes=[
            pltpu.VMEM((2, FIELDS, ring, EDGE, ROWS, LANES), f32),
            pltpu.VMEM((2, FIELDS, ring, 2 + EDGE, ROWS, LANES), f32),
            pltpu.VMEM((FIELDS, 2, blocks, ROWS * ROWS, LANES), f32),
            pltpu.SemaphoreType.DMA((FIELDS, 2)),
            pltpu.SemaphoreType.DMA((FIELDS,)),
        ],
        compiler_params=params,
        cost_estimate=pl.CostEstimate(flops=0, bytes_accessed=10**6, transcendentals=0),
    )(raw, stepped, result, places, rates, even_in, odd_in, even_other, odd_other)
    return tuple(block_of(r, side)[None] for r in results)


def solution(mesh):
    layers, cores = mesh.shape["slab"], mesh.shape["bal"]
    split, copied = P("slab", "bal", None, None), P()
    return jax.shard_map(
        functools.partial(body, layers, cores),
        mesh=mesh,
        in_specs=(split,) * 3 + (copied,) * 3,
        out_specs=(split,) * 3,
        check_vma=False,
    )
```

```python
import functools

import jax
import jax.numpy as jnp
from jax import lax
from jax.experimental import pallas as pl
from jax.experimental.pallas import tpu as pltpu
from jax.sharding import PartitionSpec as P

RATE = 0.1
ANISO = 0.05
COUPLE = 0.5
DIFF_SOLUTE = 0.08
DIFF_HEAT = 0.15
TINY = 0.0001
ROWS, LANES = 8, 128
EDGE = 2
FIELDS = 3
AXES = ("slab", "bal")
CHUNK_FIRST = 4
SHIFTED_EARLY = 1
CHUNK_SECOND = 28
VMEM_BYTES = 40 * 2**20


def tiles_of(block):
    blocks, side, cells = block.shape
    split = block.reshape(blocks, side // ROWS, ROWS, cells // LANES, LANES)
    return split.transpose(0, 1, 3, 2, 4).reshape(blocks, side * cells // LANES, LANES)


def tile_grid(block):
    blocks, side, cells = block.shape
    split = block.reshape(blocks, side // ROWS, ROWS, cells // LANES, LANES)
    return split.transpose(0, 1, 3, 2, 4)


def block_of(tiles, side):
    blocks, rows, _ = tiles.shape
    columns = rows // side
    split = tiles.reshape(blocks, side // ROWS, columns, ROWS, LANES)
    return split.transpose(0, 1, 3, 2, 4).reshape(blocks, side, columns * LANES)


def plane_rows(x):
    return pl.ds((x >> 3) * ROWS * ROWS + (x & (ROWS - 1)), ROWS, stride=ROWS)


def lane_ids():
    return lax.broadcasted_iota(jnp.int32, (ROWS, LANES), 1)


class Geometry:
    def __init__(self, side):
        lanes = lane_ids()
        self.side = side
        self.y_last = lanes >= LANES - side
        self.y_first = lanes < side
        self.z_first = lanes % side == 0
        self.z_last = lanes % side == side - 1

    def up(self, plane):
        return pltpu.roll(plane, LANES - self.side, 1)

    def down(self, plane):
        return pltpu.roll(plane, self.side, 1)

    def y_pair(self, up, down):
        upper = jnp.where(self.y_last, pltpu.roll(up, ROWS - 1, 0), up)
        lower = jnp.where(self.y_first, pltpu.roll(down, 1, 0), down)
        return upper, lower

    def z_pair(self, plane, next_down, previous_up):
        upper = pltpu.roll(jnp.where(self.z_first, next_down, plane), LANES - 1, 1)
        lower = pltpu.roll(jnp.where(self.z_last, previous_up, plane), 1, 1)
        return upper, lower


def advance(centers, sums, differences, rate):
    phase, solute, heat = centers
    sum_phase, sum_solute, sum_heat = sums
    squares = [d * d for d in differences]
    square = squares[0] + squares[1] + squares[2]
    quartic = squares[0] * squares[0] + squares[1] * squares[1] + squares[2] * squares[2]
    below = square * square + 16.0 * TINY
    anisotropy = (1.0 - 3.0 * ANISO) + 4.0 * ANISO * (quartic / below)
    well = 1.0 - phase * phase
    forcing = well * (phase - COUPLE * well * (solute + heat))
    change = rate * (anisotropy * anisotropy * (sum_phase - 6.0 * phase) + forcing)
    half = 0.5 * change
    return (
        phase + change,
        (1.0 - 6.0 * DIFF_SOLUTE) * solute + (DIFF_SOLUTE * sum_solute + half),
        (1.0 - 6.0 * DIFF_HEAT) * heat + (DIFF_HEAT * sum_heat + half),
    )


def sides(geometry, center, up, down, next_down, previous_up, phase):
    y_upper, y_lower = geometry.y_pair(up, down)
    z_upper, z_lower = geometry.z_pair(center, next_down, previous_up)
    total = (y_upper + y_lower) + (z_upper + z_lower)
    return (total, y_upper - y_lower, z_upper - z_lower) if phase else (total,)


def keep_sides(geometry, around, b, x, center, up, down, next_down, previous_up):
    for f in range(FIELDS):
        found = sides(geometry, center(f), up(f), down(f), next_down(f), previous_up(f), f == 0)
        for k, value in enumerate(found):
            around[f if k == 0 else FIELDS - 1 + k, b, x] = value


def finish(below, center, above, around, rate):
    sums = [(above[f] + below[f]) + around[f] for f in range(FIELDS)]
    return advance(center, sums, (above[0] - below[0], around[FIELDS], around[FIELDS + 1]), rate)


def planes_at(ref, p, x):
    return [ref[f, p, x] for f in range(FIELDS)]


def rate_of(active):
    return jnp.where(active != 0, jnp.float32(RATE), jnp.float32(0.0))


def start_tables(tables, held, sem):
    copies = [pltpu.make_async_copy(t, h, sem.at[i]) for i, (t, h) in enumerate(zip(tables, held))]
    for copy in copies:
        copy.start()
    return copies


def holders(before, layer, core, blocks, cores):
    found = [0] * (blocks * cores)
    for place in range(blocks * cores):
        owner = core if place < blocks else cores - 1 - core
        at = before[owner * blocks + place % blocks, layer]
        found = [jnp.where(at == p, place, found[p]) for p in range(len(found))]
    return found


def pack_kernel(side, *refs):
    grids, (even_ref, odd_ref, sem) = refs[:FIELDS], refs[FIELDS:]

    def faces(upper_ref, lower_ref):
        return [
            pltpu.make_async_copy(grids[f].at[:, row // ROWS, :, row % ROWS, :], ref.at[f, :, d], sem.at[f, end, d])
            for f in range(FIELDS)
            for d in range(EDGE)
            for end, ref, row in ((0, lower_ref, d), (1, upper_ref, side - 1 - d))
        ]

    is_even = lax.rem(lax.axis_index("slab"), 2) == 0

    @pl.when(is_even)
    def _():
        for copy in faces(even_ref, odd_ref):
            copy.start()

    @pl.when(jnp.logical_not(is_even))
    def _():
        for copy in faces(odd_ref, even_ref):
            copy.start()

    for copy in faces(even_ref, odd_ref):
        copy.wait()


def spread(geometry, planes, slots, own, others, raw, ups, downs):
    blocks = own.shape[1]
    for x in planes:
        for f in range(FIELDS):
            for k in slots:
                source = own.at[f] if k < blocks else others[f]
                plane = source[k % blocks, plane_rows(x)]
                raw[f, k, x] = plane
                ups[f, k, x] = geometry.up(plane)
                downs[f, k, x] = geometry.down(plane)


def early_kernel(side, blocks, cores, *refs):
    fields, others = refs[:FIELDS], refs[FIELDS : 2 * FIELDS]
    raw, ups, downs, own, own_sem = refs[2 * FIELDS :]

    @pl.when(lax.axis_index("slab") == 0)
    def _():
        own_copies = [pltpu.make_async_copy(fields[f], own.at[f], own_sem.at[f]) for f in range(FIELDS)]
        for copy in own_copies:
            copy.start()
        geometry = Geometry(side)
        spread(geometry, range(side), range(blocks, blocks * cores), own, others, raw, ups, downs)
        for copy in own_copies:
            copy.wait()
        spread(geometry, range(side), range(blocks), own, others, raw, ups, downs)


def first_kernel(side, blocks, cores, layers, *refs):
    fields, others, tables = refs[:FIELDS], refs[FIELDS : 2 * FIELDS], refs[2 * FIELDS : 2 * FIELDS + 3]
    outs, scratch = refs[2 * FIELDS + 6 : 2 * FIELDS + 15], refs[2 * FIELDS + 15 :]
    raw, ups, downs, stepped, next_ups, next_downs, face_around, places_out, rates_out = outs
    own, around, before, after, flags, own_sem, table_sem = scratch
    ring = blocks * cores
    layer, core = lax.axis_index("slab"), lax.axis_index("bal")
    is_spread = layer == 0
    own_copies = [pltpu.make_async_copy(fields[f], own.at[f], own_sem.at[f]) for f in range(FIELDS)]

    @pl.when(jnp.logical_not(is_spread))
    def _():
        for copy in own_copies:
            copy.start()

    table_copies = start_tables(tables, (before, after, flags), table_sem)
    geometry = Geometry(side)

    @pl.when(jnp.logical_not(is_spread))
    def _():
        spread(geometry, range(side), range(blocks, ring), own, others, raw, ups, downs)
        for copy in own_copies:
            copy.wait()
        spread(geometry, range(CHUNK_FIRST), range(blocks), own, others, raw, ups, downs)

    for copy in table_copies:
        copy.wait()
    beside = [jnp.clip(layer + 2 * end - 1, 0, layers - 1) for end in range(2)]
    places = holders(before, layer, core, blocks, cores)
    listed = places + [after[core * blocks + b, layer] for b in range(blocks)]
    for table in beside:
        for c in range(cores):
            slot = jnp.where(c == 0, core, cores - 1 - core) * blocks
            listed += [before[slot + b, table] for b in range(blocks)]
    for k, place in enumerate(listed):
        places_out[k] = jnp.full((ROWS, LANES), place, jnp.int32)
    rates = [rate_of(flags[p, table]) for table in [layer] + beside for p in range(ring)]
    for k, rate in enumerate(rates):
        rates_out[k] = jnp.full((ROWS, LANES), rate, jnp.float32)

    def gather(planes):
        for x in planes:
            face = x in (0, side - 1)
            for p in range(ring):
                here, following, previous = places[p], places[(p + 1) % ring], places[(p - 1) % ring]
                keep_sides(
                    geometry,
                    face_around if face else around,
                    p,
                    x // (side - 1) if face else x,
                    lambda f: raw[f, here, x],
                    lambda f: ups[f, here, x],
                    lambda f: downs[f, here, x],
                    lambda f: downs[f, following, x],
                    lambda f: ups[f, previous, x],
                )

    def calculate(planes):
        for x in planes:
            for p in range(ring):
                low, center, high = (planes_at(raw, places[p], x + d) for d in (-1, 0, 1))
                new = finish(low, center, high, [around[k, p, x] for k in range(FIELDS + 2)], rates[p])
                for f in range(FIELDS):
                    stepped[f, p, x] = new[f]
                    if f < SHIFTED_EARLY:
                        next_ups[f, p, x] = geometry.up(new[f])
                        next_downs[f, p, x] = geometry.down(new[f])

    def steps(spread_too):
        count = side // CHUNK_FIRST
        for c in range(count):
            planes = range(c * CHUNK_FIRST, (c + 1) * CHUNK_FIRST)
            gather(planes)
            if spread_too and c + 1 < count:
                ahead = [x + CHUNK_FIRST for x in planes]
                spread(geometry, ahead, range(blocks), own, others, raw, ups, downs)
            calculate([x for x in planes if 0 < x < side - 1])

    pl.when(is_spread)(lambda: steps(False))
    pl.when(jnp.logical_not(is_spread))(lambda: steps(True))


def place_at(ref, k):
    return ref[k][0, 0]


def second_kernel(side, blocks, cores, *refs):
    stepped, ups, downs, places_ref, rates_ref, result, rim_around, shifted, around = refs
    ring = blocks * cores
    geometry = Geometry(side)
    places = [place_at(places_ref, ring + b) for b in range(blocks)]
    rates = [rates_ref[p] for p in places]

    rounds = [(p, (p + 1) & (ring - 1), (p + ring - 1) & (ring - 1)) for p in places]

    def shift(x):
        for b, (p, following, previous) in enumerate(rounds):
            for f in range(SHIFTED_EARLY, FIELDS):
                shifted[0, f, b, x] = geometry.up(stepped[f, p, x])
                shifted[1, f, b, x] = geometry.down(stepped[f, p, x])
                shifted[2, f, b, x] = geometry.down(stepped[f, following, x])
                shifted[3, f, b, x] = geometry.up(stepped[f, previous, x])

    def gather(x, target, at):
        for b, (p, following, previous) in enumerate(rounds):
            keep_sides(
                geometry,
                target,
                b,
                at,
                lambda f: stepped[f, p, x],
                lambda f: ups[f, p, x] if f < SHIFTED_EARLY else shifted[0, f, b, x],
                lambda f: downs[f, p, x] if f < SHIFTED_EARLY else shifted[1, f, b, x],
                lambda f: downs[f, following, x] if f < SHIFTED_EARLY else shifted[2, f, b, x],
                lambda f: ups[f, previous, x] if f < SHIFTED_EARLY else shifted[3, f, b, x],
            )

    @pl.loop(0, (side - 4) // CHUNK_SECOND)
    def _(i):
        planes = [2 + i * CHUNK_SECOND + u for u in range(CHUNK_SECOND)]
        for x in planes:
            shift(x)
        for x in planes:
            gather(x, around, x)
        for x in planes:
            for b, p in enumerate(places):
                low, center, high = (planes_at(stepped, p, x + d) for d in (-1, 0, 1))
                new = finish(low, center, high, [around[k, b, x] for k in range(FIELDS + 2)], rates[b])
                for f in range(FIELDS):
                    result[f, b, plane_rows(x)] = new[f]

    for end in range(2):
        shift(1 + end * (side - 3))
    for end in range(2):
        gather(1 + end * (side - 3), rim_around, end)


def rim_kernel(side, blocks, cores, layers, *refs):
    raw, inner, result, face_around, rim_around, places_ref, rates_ref = refs[:7]
    messages = refs[7:11]
    outs = refs[11 : 11 + FIELDS]
    halo, faces, shifted, around, tiles, sem, middle_sem = refs[11 + FIELDS :]
    ring = blocks * cores
    layer = lax.axis_index("slab")
    parity = lax.rem(layer, 2)
    geometry = Geometry(side)
    rows = ROWS * ROWS
    middle = pl.ds(rows, side * ROWS - 2 * rows)
    copies = [
        pltpu.make_async_copy(result.at[f, :, middle], outs[f].at[:, middle], middle_sem.at[f])
        for f in range(FIELDS)
    ]
    for copy in copies:
        copy.start()
    places = [place_at(places_ref, p) for p in range(ring)]
    targets = [place_at(places_ref, ring + b) for b in range(blocks)]
    beside = [layer + 2 * end - 1 for end in range(2)]
    outside = [jnp.logical_or(b < 0, b >= layers) for b in beside]
    ends = range(2)

    def at_face(end, p, d):
        return planes_at(raw, places[p], d if end == 0 else side - 1 - d)

    for end in ends:
        from_even = parity == 1 - end
        for c in range(cores):
            for b in range(blocks):
                p = place_at(places_ref, ring + blocks + (end * cores + c) * blocks + b)
                for f in range(FIELDS):
                    for d in range(EDGE):
                        halo[end, f, p, d] = jnp.where(
                            from_even, messages[2 * c][f, b, d], messages[2 * c + 1][f, b, d]
                        )
    for f in range(FIELDS):
        for end in ends:
            tiles[f, end] = result[f, :, pl.ds(end * (side * ROWS - rows), rows)]
    for end in ends:
        for p in range(ring):
            for f in range(FIELDS):
                near = jnp.where(outside[end], at_face(end, p, 0)[f], halo[end, f, p, 0])
                halo[end, f, p, 0] = near
                shifted[0, end, f, p] = geometry.up(near)
                shifted[1, end, f, p] = geometry.down(near)
    for end in ends:
        for p in range(ring):
            new = finish(
                [halo[end, f, p, 0] for f in range(FIELDS)],
                at_face(end, p, 0),
                at_face(end, p, 1),
                [face_around[k, p, end] for k in range(FIELDS + 2)],
                rates_ref[p],
            )
            for f in range(FIELDS):
                faces[end, f, p, 1] = new[f]
    for end in ends:
        for p in range(ring):
            keep_sides(
                geometry,
                around,
                p,
                end,
                lambda f: halo[end, f, p, 0],
                lambda f: shifted[0, end, f, p],
                lambda f: shifted[1, end, f, p],
                lambda f: shifted[1, end, f, (p + 1) % ring],
                lambda f: shifted[0, end, f, (p - 1) % ring],
            )
    rounds = [(p, (p + 1) & (ring - 1), (p + ring - 1) & (ring - 1)) for p in targets]
    for end in ends:
        for b, (p, following, previous) in enumerate(rounds):
            for f in range(FIELDS):
                shifted[2, end, f, 4 * b] = geometry.up(faces[end, f, p, 1])
                shifted[2, end, f, 4 * b + 1] = geometry.down(faces[end, f, p, 1])
                shifted[2, end, f, 4 * b + 2] = geometry.down(faces[end, f, following, 1])
                shifted[2, end, f, 4 * b + 3] = geometry.up(faces[end, f, previous, 1])
    for end in ends:
        for p in range(ring):
            new = finish(
                [halo[end, f, p, 1] for f in range(FIELDS)],
                [halo[end, f, p, 0] for f in range(FIELDS)],
                at_face(end, p, 0),
                [around[k, p, end] for k in range(FIELDS + 2)],
                rates_ref[ring * (1 + end) + p],
            )
            for f in range(FIELDS):
                faces[end, f, p, 0] = jnp.where(outside[end], faces[end, f, p, 1], new[f])
    for end in ends:
        for b, (p, following, previous) in enumerate(rounds):
            keep_sides(
                geometry,
                around,
                ring + b,
                end,
                lambda f: faces[end, f, p, 1],
                lambda f: shifted[2, end, f, 4 * b],
                lambda f: shifted[2, end, f, 4 * b + 1],
                lambda f: shifted[2, end, f, 4 * b + 2],
                lambda f: shifted[2, end, f, 4 * b + 3],
            )
    for end in ends:
        for b, p in enumerate(targets):
            outer, face = ([faces[end, f, p, d] for f in range(FIELDS)] for d in range(2))
            first, second = (planes_at(inner, p, d if end == 0 else side - 1 - d) for d in (1, 2))
            news = (
                finish(outer, face, first, [around[k, ring + b, end] for k in range(FIELDS + 2)], rates_ref[p]),
                finish(face, first, second, [rim_around[k, b, end] for k in range(FIELDS + 2)], rates_ref[p]),
            )
            for d in range(EDGE):
                row = d if end == 0 else ROWS - 1 - d
                for f in range(FIELDS):
                    tiles[f, end, b, pl.ds(row, ROWS, stride=ROWS)] = news[d][f]
        for f in range(FIELDS):
            part = pl.ds(end * (side * ROWS - rows), rows)
            copies.append(pltpu.make_async_copy(tiles.at[f, end], outs[f].at[:, part], sem.at[f, end]))
            copies[-1].start()
    for copy in copies:
        copy.wait()


def neighbour_swaps(layers, cores, first):
    pairs = []
    for layer in range(layers):
        partner = layer + 1 if (layer - first) % 2 == 0 else layer - 1
        for core in range(cores):
            here = layer * cores + core
            if 0 <= partner < layers:
                pairs.append((here, partner * cores + core))
            else:
                pairs.append((here, layer * cores + cores - 1 - core))
    return pairs


def body(layers, cores, order_parameter, concentration_excess, thermal_subcooling, before, after, flags):
    blocks, side = order_parameter.shape[1], order_parameter.shape[2]
    ring = blocks * cores
    rows = side * ROWS
    f32 = jnp.float32
    before, after, flags = before.T, after.T, flags.T
    owners = [(s * cores + c, s * cores + cores - 1 - c) for s in range(layers) for c in range(cores)]
    fields = [tiles_of(a[0]) for a in (order_parameter, concentration_excess, thermal_subcooling)]
    others = [lax.ppermute(a, AXES, owners) for a in fields]
    vmem, hbm = (pl.BlockSpec(memory_space=m) for m in (pltpu.VMEM, pltpu.HBM))
    params = pltpu.CompilerParams(vmem_limit_bytes=VMEM_BYTES)
    message = jax.ShapeDtypeStruct((FIELDS, blocks, EDGE, ROWS, LANES), f32)
    table = pltpu.SMEM(before.shape, jnp.int32)
    in_hbm = lambda *arrays: [pltpu.with_memory_space_constraint(a, pltpu.HBM) for a in arrays]
    grids = [tile_grid(a[0]) for a in (order_parameter, concentration_excess, thermal_subcooling)]
    even, odd = pl.pallas_call(
        functools.partial(pack_kernel, side),
        out_shape=(message, message),
        in_specs=[hbm] * FIELDS,
        out_specs=(vmem,) * 2,
        scratch_shapes=[pltpu.SemaphoreType.DMA((FIELDS, 2, EDGE))],
        compiler_params=params,
        cost_estimate=pl.CostEstimate(flops=0, bytes_accessed=10**6, transcendentals=0),
    )(*in_hbm(*grids))
    planes = (FIELDS, ring, side, ROWS, LANES)
    kept = FIELDS + 2
    three = (jax.ShapeDtypeStruct(planes, f32),) * 3
    own_scratch = pltpu.VMEM((FIELDS, blocks, rows, LANES), f32)
    odd_in = lax.ppermute(odd, AXES, neighbour_swaps(layers, cores, 1))
    early = pl.pallas_call(
        functools.partial(early_kernel, side, blocks, cores),
        out_shape=three,
        in_specs=[hbm] * FIELDS + [vmem] * FIELDS,
        out_specs=(vmem,) * 3,
        scratch_shapes=[own_scratch, pltpu.SemaphoreType.DMA((FIELDS,))],
        compiler_params=params,
        cost_estimate=pl.CostEstimate(flops=0, bytes_accessed=10**6, transcendentals=0),
    )(*in_hbm(*fields), *others)
    even, *early = lax.optimization_barrier((even, *early))
    even_in = lax.ppermute(even, AXES, neighbour_swaps(layers, cores, 0))
    raw, _, _, stepped, ups, downs, face_around, places, rates = pl.pallas_call(
        functools.partial(first_kernel, side, blocks, cores, layers),
        out_shape=three * 2
        + (
            jax.ShapeDtypeStruct((kept, ring, 2, ROWS, LANES), f32),
            jax.ShapeDtypeStruct((3 * ring + blocks, ROWS, LANES), jnp.int32),
            jax.ShapeDtypeStruct((3 * ring, ROWS, LANES), f32),
        ),
        in_specs=[hbm] * FIELDS + [vmem] * FIELDS + [hbm] * 3 + [vmem] * 3,
        out_specs=(vmem,) * 9,
        input_output_aliases={2 * FIELDS + 3 + k: k for k in range(3)},
        scratch_shapes=[own_scratch, pltpu.VMEM((kept, ring, side, ROWS, LANES), f32)]
        + [table] * 3
        + [pltpu.SemaphoreType.DMA((FIELDS,)), pltpu.SemaphoreType.DMA((3,))],
        compiler_params=params,
        cost_estimate=pl.CostEstimate(flops=0, bytes_accessed=10**7, transcendentals=0),
    )(*in_hbm(*fields), *others, *in_hbm(before, after, flags), *early)
    odd_in, even_in, stepped = lax.optimization_barrier((odd_in, even_in, stepped))
    odd_other = lax.ppermute(odd_in, AXES, owners)
    even_other = lax.ppermute(even_in, AXES, owners)
    result, rim_around = pl.pallas_call(
        functools.partial(second_kernel, side, blocks, cores),
        out_shape=(
            jax.ShapeDtypeStruct((FIELDS, blocks, rows, LANES), f32),
            jax.ShapeDtypeStruct((kept, blocks, 2, ROWS, LANES), f32),
        ),
        in_specs=[vmem] * 5,
        out_specs=(vmem,) * 2,
        scratch_shapes=[
            pltpu.VMEM((4, FIELDS, blocks, side, ROWS, LANES), f32),
            pltpu.VMEM((kept, blocks, side, ROWS, LANES), f32),
        ],
        compiler_params=params,
        cost_estimate=pl.CostEstimate(flops=0, bytes_accessed=10**7, transcendentals=0),
    )(stepped, ups, downs, places, rates)
    results = pl.pallas_call(
        functools.partial(rim_kernel, side, blocks, cores, layers),
        out_shape=(jax.ShapeDtypeStruct((blocks, rows, LANES), f32),) * FIELDS,
        in_specs=[vmem] * 11,
        out_specs=(hbm,) * FIELDS,
        scratch_shapes=[
            pltpu.VMEM((2, FIELDS, ring, EDGE, ROWS, LANES), f32),
            pltpu.VMEM((2, FIELDS, ring, 2, ROWS, LANES), f32),
            pltpu.VMEM((3, 2, FIELDS, max(ring, 4 * blocks), ROWS, LANES), f32),
            pltpu.VMEM((kept, ring + blocks, 2, ROWS, LANES), f32),
            pltpu.VMEM((FIELDS, 2, blocks, ROWS * ROWS, LANES), f32),
            pltpu.SemaphoreType.DMA((FIELDS, 2)),
            pltpu.SemaphoreType.DMA((FIELDS,)),
        ],
        compiler_params=params,
        cost_estimate=pl.CostEstimate(flops=0, bytes_accessed=10**6, transcendentals=0),
    )(raw, stepped, result, face_around, rim_around, places, rates, even_in, odd_in, even_other, odd_other)
    return tuple(block_of(r, side)[None] for r in results)


def solution(mesh):
    layers, cores = mesh.shape["slab"], mesh.shape["bal"]
    split, copied = P("slab", "bal", None, None), P()
    return jax.shard_map(
        functools.partial(body, layers, cores),
        mesh=mesh,
        in_specs=(split,) * 3 + (copied,) * 3,
        out_specs=(split,) * 3,
        check_vma=False,
    )
```

```python
import functools

import jax
import jax.numpy as jnp
from jax import lax
from jax.experimental import pallas as pl
from jax.experimental.pallas import tpu as pltpu
from jax.sharding import PartitionSpec as P

RATE = 0.1
ANISO = 0.05
COUPLE = 0.5
DIFF_SOLUTE = 0.08
DIFF_HEAT = 0.15
TINY = 0.0001
ROWS, LANES = 8, 128
EDGE = 2
FIELDS = 3
AXES = ("slab", "bal")
CHUNK_FIRST = 4
SHIFTED_EARLY = 2
CHUNK_SECOND = 28
VMEM_BYTES = 40 * 2**20


def tiles_of(block):
    blocks, side, cells = block.shape
    split = block.reshape(blocks, side // ROWS, ROWS, cells // LANES, LANES)
    return split.transpose(0, 1, 3, 2, 4).reshape(blocks, side * cells // LANES, LANES)


def block_of(tiles, side):
    blocks, rows, _ = tiles.shape
    columns = rows // side
    split = tiles.reshape(blocks, side // ROWS, columns, ROWS, LANES)
    return split.transpose(0, 1, 3, 2, 4).reshape(blocks, side, columns * LANES)


def plane_rows(x):
    return pl.ds((x >> 3) * ROWS * ROWS + (x & (ROWS - 1)), ROWS, stride=ROWS)


def lane_ids():
    return lax.broadcasted_iota(jnp.int32, (ROWS, LANES), 1)


class Geometry:
    def __init__(self, side):
        lanes = lane_ids()
        self.side = side
        self.y_last = lanes >= LANES - side
        self.y_first = lanes < side
        self.z_first = lanes % side == 0
        self.z_last = lanes % side == side - 1

    def up(self, plane):
        return pltpu.roll(plane, LANES - self.side, 1)

    def down(self, plane):
        return pltpu.roll(plane, self.side, 1)

    def y_pair(self, up, down):
        upper = jnp.where(self.y_last, pltpu.roll(up, ROWS - 1, 0), up)
        lower = jnp.where(self.y_first, pltpu.roll(down, 1, 0), down)
        return upper, lower

    def z_pair(self, plane, next_down, previous_up):
        upper = pltpu.roll(jnp.where(self.z_first, next_down, plane), LANES - 1, 1)
        lower = pltpu.roll(jnp.where(self.z_last, previous_up, plane), 1, 1)
        return upper, lower


def advance(centers, sums, differences, rate):
    phase, solute, heat = centers
    sum_phase, sum_solute, sum_heat = sums
    squares = [d * d for d in differences]
    square = squares[0] + squares[1] + squares[2]
    quartic = squares[0] * squares[0] + squares[1] * squares[1] + squares[2] * squares[2]
    below = square * square + 16.0 * TINY
    anisotropy = (1.0 - 3.0 * ANISO) + 4.0 * ANISO * (quartic / below)
    well = 1.0 - phase * phase
    forcing = well * (phase - COUPLE * well * (solute + heat))
    change = rate * (anisotropy * anisotropy * (sum_phase - 6.0 * phase) + forcing)
    half = 0.5 * change
    return (
        phase + change,
        (1.0 - 6.0 * DIFF_SOLUTE) * solute + (DIFF_SOLUTE * sum_solute + half),
        (1.0 - 6.0 * DIFF_HEAT) * heat + (DIFF_HEAT * sum_heat + half),
    )


def sides(geometry, center, up, down, next_down, previous_up, phase):
    y_upper, y_lower = geometry.y_pair(up, down)
    z_upper, z_lower = geometry.z_pair(center, next_down, previous_up)
    total = (y_upper + y_lower) + (z_upper + z_lower)
    return (total, y_upper - y_lower, z_upper - z_lower) if phase else (total,)


def keep_sides(geometry, around, b, x, center, up, down, next_down, previous_up):
    for f in range(FIELDS):
        found = sides(geometry, center(f), up(f), down(f), next_down(f), previous_up(f), f == 0)
        for k, value in enumerate(found):
            around[f if k == 0 else FIELDS - 1 + k, b, x] = value


def finish(below, center, above, around, rate):
    sums = [(above[f] + below[f]) + around[f] for f in range(FIELDS)]
    return advance(center, sums, (above[0] - below[0], around[FIELDS], around[FIELDS + 1]), rate)


def planes_at(ref, p, x):
    return [ref[f, p, x] for f in range(FIELDS)]


def rate_of(active):
    return jnp.where(active != 0, jnp.float32(RATE), jnp.float32(0.0))


def start_tables(tables, held, sem):
    copies = [pltpu.make_async_copy(t, h, sem.at[i]) for i, (t, h) in enumerate(zip(tables, held))]
    for copy in copies:
        copy.start()
    return copies


def holders(before, layer, core, blocks, cores):
    found = [0] * (blocks * cores)
    for place in range(blocks * cores):
        owner = core if place < blocks else cores - 1 - core
        at = before[owner * blocks + place % blocks, layer]
        found = [jnp.where(at == p, place, found[p]) for p in range(len(found))]
    return found


def pack_kernel(side, blocks, cores, layers, *refs):
    fields, tables = refs[:FIELDS], refs[FIELDS : FIELDS + 3]
    even_ref, odd_ref, own, places_out, rates_out = refs[FIELDS + 3 : FIELDS + 8]
    before, after, flags, own_sem, table_sem = refs[FIELDS + 8 :]
    ring = blocks * cores
    layer, core = lax.axis_index("slab"), lax.axis_index("bal")
    own_copies = [pltpu.make_async_copy(fields[f], own.at[f], own_sem.at[f]) for f in range(FIELDS)]
    for copy in own_copies:
        copy.start()
    copies = start_tables(tables, (before, after, flags), table_sem)
    for copy in copies:
        copy.wait()
    beside = [jnp.clip(layer + 2 * end - 1, 0, layers - 1) for end in range(2)]
    listed = holders(before, layer, core, blocks, cores)
    listed += [after[core * blocks + b, layer] for b in range(blocks)]
    for table in beside:
        for c in range(cores):
            slot = jnp.where(c == 0, cores - 1 - core, core) * blocks
            listed += [before[slot + b, table] for b in range(blocks)]
    for k, place in enumerate(listed):
        places_out[k] = jnp.full((ROWS, LANES), place, jnp.int32)
    rates = [rate_of(flags[p, table]) for table in [layer] + beside for p in range(ring)]
    for k, rate in enumerate(rates):
        rates_out[k] = jnp.full((ROWS, LANES), rate, jnp.float32)
    is_even = lax.rem(layer, 2) == 0
    for f in range(FIELDS):
        own_copies[f].wait()
        for b in range(blocks):
            for d in range(EDGE):
                lower, upper = own[f, b, plane_rows(d)], own[f, b, plane_rows(side - 1 - d)]
                even_ref[f, b, d] = jnp.where(is_even, upper, lower)
                odd_ref[f, b, d] = jnp.where(is_even, lower, upper)


def first_kernel(side, blocks, cores, *refs):
    own, other, places_ref, rates_ref = refs[:4]
    raw, stepped, next_ups, next_downs, face_around, ups, downs, around = refs[4:]
    ring = blocks * cores
    geometry = Geometry(side)
    places = [place_at(places_ref, p) for p in range(ring)]
    rates = [rates_ref[p] for p in range(ring)]

    def spread(planes):
        for x in planes:
            for f in range(FIELDS):
                for k in range(ring):
                    source = own if k < blocks else other
                    plane = source[f, k % blocks, plane_rows(x)]
                    raw[f, k, x] = plane
                    ups[f, k, x] = geometry.up(plane)
                    downs[f, k, x] = geometry.down(plane)

    def gather(planes):
        for x in planes:
            face = x in (0, side - 1)
            for p in range(ring):
                here, following, previous = places[p], places[(p + 1) % ring], places[(p - 1) % ring]
                keep_sides(
                    geometry,
                    face_around if face else around,
                    p,
                    x // (side - 1) if face else x,
                    lambda f: raw[f, here, x],
                    lambda f: ups[f, here, x],
                    lambda f: downs[f, here, x],
                    lambda f: downs[f, following, x],
                    lambda f: ups[f, previous, x],
                )

    def calculate(planes):
        for x in planes:
            for p in range(ring):
                low, center, high = (planes_at(raw, places[p], x + d) for d in (-1, 0, 1))
                new = finish(low, center, high, [around[k, p, x] for k in range(FIELDS + 2)], rates[p])
                for f in range(FIELDS):
                    stepped[f, p, x] = new[f]
                    if f < SHIFTED_EARLY:
                        next_ups[f, p, x] = geometry.up(new[f])
                        next_downs[f, p, x] = geometry.down(new[f])

    count = side // CHUNK_FIRST
    spread(range(CHUNK_FIRST))
    for c in range(count):
        planes = range(c * CHUNK_FIRST, (c + 1) * CHUNK_FIRST)
        gather(planes)
        if c + 1 < count:
            spread([x + CHUNK_FIRST for x in planes])
        calculate([x for x in planes if 0 < x < side - 1])


def place_at(ref, k):
    return ref[k][0, 0]


def second_kernel(side, blocks, cores, *refs):
    stepped, ups, downs, places_ref, rates_ref, result, rim_around, shifted, around = refs
    ring = blocks * cores
    geometry = Geometry(side)
    places = [place_at(places_ref, ring + b) for b in range(blocks)]
    rates = [rates_ref[p] for p in places]

    rounds = [(p, (p + 1) & (ring - 1), (p + ring - 1) & (ring - 1)) for p in places]

    def shift(x):
        for b, (p, following, previous) in enumerate(rounds):
            for f in range(SHIFTED_EARLY, FIELDS):
                shifted[0, f, b, x] = geometry.up(stepped[f, p, x])
                shifted[1, f, b, x] = geometry.down(stepped[f, p, x])
                shifted[2, f, b, x] = geometry.down(stepped[f, following, x])
                shifted[3, f, b, x] = geometry.up(stepped[f, previous, x])

    def gather(x, target, at):
        for b, (p, following, previous) in enumerate(rounds):
            keep_sides(
                geometry,
                target,
                b,
                at,
                lambda f: stepped[f, p, x],
                lambda f: ups[f, p, x] if f < SHIFTED_EARLY else shifted[0, f, b, x],
                lambda f: downs[f, p, x] if f < SHIFTED_EARLY else shifted[1, f, b, x],
                lambda f: downs[f, following, x] if f < SHIFTED_EARLY else shifted[2, f, b, x],
                lambda f: ups[f, previous, x] if f < SHIFTED_EARLY else shifted[3, f, b, x],
            )

    @pl.loop(0, (side - 4) // CHUNK_SECOND)
    def _(i):
        planes = [2 + i * CHUNK_SECOND + u for u in range(CHUNK_SECOND)]
        for x in planes:
            shift(x)
        for x in planes:
            gather(x, around, x)
        for x in planes:
            for b, p in enumerate(places):
                low, center, high = (planes_at(stepped, p, x + d) for d in (-1, 0, 1))
                new = finish(low, center, high, [around[k, b, x] for k in range(FIELDS + 2)], rates[b])
                for f in range(FIELDS):
                    result[f, b, plane_rows(x)] = new[f]

    for end in range(2):
        shift(1 + end * (side - 3))
    for end in range(2):
        gather(1 + end * (side - 3), rim_around, end)


def rim_kernel(side, blocks, cores, layers, *refs):
    raw, inner, result, face_around, rim_around, places_ref, rates_ref = refs[:7]
    messages = refs[7:9]
    outs = refs[9 : 9 + FIELDS]
    halo, faces, shifted, around, tiles, sem, middle_sem = refs[9 + FIELDS :]
    ring = blocks * cores
    layer = lax.axis_index("slab")
    parity = lax.rem(layer, 2)
    geometry = Geometry(side)
    rows = ROWS * ROWS
    middle = pl.ds(rows, side * ROWS - 2 * rows)
    copies = [
        pltpu.make_async_copy(result.at[f, :, middle], outs[f].at[:, middle], middle_sem.at[f])
        for f in range(FIELDS)
    ]
    for copy in copies:
        copy.start()
    places = [place_at(places_ref, p) for p in range(ring)]
    targets = [place_at(places_ref, ring + b) for b in range(blocks)]
    beside = [layer + 2 * end - 1 for end in range(2)]
    outside = [jnp.logical_or(b < 0, b >= layers) for b in beside]
    ends = range(2)

    def at_face(end, p, d):
        return planes_at(raw, places[p], d if end == 0 else side - 1 - d)

    for end in ends:
        message = jnp.where(parity == 1 - end, 0, 1)
        for c in range(cores):
            for b in range(blocks):
                p = place_at(places_ref, ring + blocks + (end * cores + c) * blocks + b)
                for f in range(FIELDS):
                    for d in range(EDGE):
                        halo[end, f, p, d] = messages[c][message, f, b, d]
    for f in range(FIELDS):
        for end in ends:
            tiles[f, end] = result[f, :, pl.ds(end * (side * ROWS - rows), rows)]
    for end in ends:
        for p in range(ring):
            for f in range(FIELDS):
                near = jnp.where(outside[end], at_face(end, p, 0)[f], halo[end, f, p, 0])
                halo[end, f, p, 0] = near
                shifted[0, end, f, p] = geometry.up(near)
                shifted[1, end, f, p] = geometry.down(near)
    for end in ends:
        for p in range(ring):
            new = finish(
                [halo[end, f, p, 0] for f in range(FIELDS)],
                at_face(end, p, 0),
                at_face(end, p, 1),
                [face_around[k, p, end] for k in range(FIELDS + 2)],
                rates_ref[p],
            )
            for f in range(FIELDS):
                faces[end, f, p, 1] = new[f]
    for end in ends:
        for p in range(ring):
            keep_sides(
                geometry,
                around,
                p,
                end,
                lambda f: halo[end, f, p, 0],
                lambda f: shifted[0, end, f, p],
                lambda f: shifted[1, end, f, p],
                lambda f: shifted[1, end, f, (p + 1) % ring],
                lambda f: shifted[0, end, f, (p - 1) % ring],
            )
    rounds = [(p, (p + 1) & (ring - 1), (p + ring - 1) & (ring - 1)) for p in targets]
    for end in ends:
        for b, (p, following, previous) in enumerate(rounds):
            for f in range(FIELDS):
                shifted[2, end, f, 4 * b] = geometry.up(faces[end, f, p, 1])
                shifted[2, end, f, 4 * b + 1] = geometry.down(faces[end, f, p, 1])
                shifted[2, end, f, 4 * b + 2] = geometry.down(faces[end, f, following, 1])
                shifted[2, end, f, 4 * b + 3] = geometry.up(faces[end, f, previous, 1])
    for end in ends:
        for p in range(ring):
            new = finish(
                [halo[end, f, p, 1] for f in range(FIELDS)],
                [halo[end, f, p, 0] for f in range(FIELDS)],
                at_face(end, p, 0),
                [around[k, p, end] for k in range(FIELDS + 2)],
                rates_ref[ring * (1 + end) + p],
            )
            for f in range(FIELDS):
                faces[end, f, p, 0] = jnp.where(outside[end], faces[end, f, p, 1], new[f])
    for end in ends:
        for b, (p, following, previous) in enumerate(rounds):
            keep_sides(
                geometry,
                around,
                ring + b,
                end,
                lambda f: faces[end, f, p, 1],
                lambda f: shifted[2, end, f, 4 * b],
                lambda f: shifted[2, end, f, 4 * b + 1],
                lambda f: shifted[2, end, f, 4 * b + 2],
                lambda f: shifted[2, end, f, 4 * b + 3],
            )
    for end in ends:
        for b, p in enumerate(targets):
            outer, face = ([faces[end, f, p, d] for f in range(FIELDS)] for d in range(2))
            first, second = (planes_at(inner, p, d if end == 0 else side - 1 - d) for d in (1, 2))
            news = (
                finish(outer, face, first, [around[k, ring + b, end] for k in range(FIELDS + 2)], rates_ref[p]),
                finish(face, first, second, [rim_around[k, b, end] for k in range(FIELDS + 2)], rates_ref[p]),
            )
            for d in range(EDGE):
                row = d if end == 0 else ROWS - 1 - d
                for f in range(FIELDS):
                    tiles[f, end, b, pl.ds(row, ROWS, stride=ROWS)] = news[d][f]
        for f in range(FIELDS):
            part = pl.ds(end * (side * ROWS - rows), rows)
            copies.append(pltpu.make_async_copy(tiles.at[f, end], outs[f].at[:, part], sem.at[f, end]))
            copies[-1].start()
    for copy in copies:
        copy.wait()


def neighbour_swaps(layers, cores, first):
    pairs = []
    for layer in range(layers):
        partner = layer + 1 if (layer - first) % 2 == 0 else layer - 1
        for core in range(cores):
            here = layer * cores + core
            if 0 <= partner < layers:
                pairs.append((here, partner * cores + cores - 1 - core))
            else:
                pairs.append((here, layer * cores + cores - 1 - core))
    return pairs


def body(layers, cores, order_parameter, concentration_excess, thermal_subcooling, before, after, flags):
    blocks, side = order_parameter.shape[1], order_parameter.shape[2]
    ring = blocks * cores
    rows = side * ROWS
    f32 = jnp.float32
    before, after, flags = before.T, after.T, flags.T
    owners = [(s * cores + c, s * cores + cores - 1 - c) for s in range(layers) for c in range(cores)]
    fields = [tiles_of(a[0]) for a in (order_parameter, concentration_excess, thermal_subcooling)]
    vmem, hbm = (pl.BlockSpec(memory_space=m) for m in (pltpu.VMEM, pltpu.HBM))
    params = pltpu.CompilerParams(vmem_limit_bytes=VMEM_BYTES)
    message = jax.ShapeDtypeStruct((FIELDS, blocks, EDGE, ROWS, LANES), f32)
    table = pltpu.SMEM(before.shape, jnp.int32)
    in_hbm = lambda *arrays: [pltpu.with_memory_space_constraint(a, pltpu.HBM) for a in arrays]
    numbers = (
        jax.ShapeDtypeStruct((3 * ring + blocks, ROWS, LANES), jnp.int32),
        jax.ShapeDtypeStruct((3 * ring, ROWS, LANES), f32),
    )
    even, odd, own, places, rates = pl.pallas_call(
        functools.partial(pack_kernel, side, blocks, cores, layers),
        out_shape=(message, message, jax.ShapeDtypeStruct((FIELDS, blocks, rows, LANES), f32)) + numbers,
        in_specs=[hbm] * (FIELDS + 3),
        out_specs=(vmem,) * 5,
        scratch_shapes=[table] * 3
        + [pltpu.SemaphoreType.DMA((FIELDS,)), pltpu.SemaphoreType.DMA((3,))],
        compiler_params=params,
        cost_estimate=pl.CostEstimate(flops=0, bytes_accessed=10**6, transcendentals=0),
    )(*in_hbm(*fields, before, after, flags))
    other = lax.ppermute(own, AXES, owners)
    odd_in = lax.ppermute(odd, AXES, neighbour_swaps(layers, cores, 1))
    even_in = lax.ppermute(even, AXES, neighbour_swaps(layers, cores, 0))
    planes = (FIELDS, ring, side, ROWS, LANES)
    kept = FIELDS + 2
    raw, stepped, ups, downs, face_around = pl.pallas_call(
        functools.partial(first_kernel, side, blocks, cores),
        out_shape=(jax.ShapeDtypeStruct(planes, f32),) * 4
        + (jax.ShapeDtypeStruct((kept, ring, 2, ROWS, LANES), f32),),
        in_specs=[vmem] * 4,
        out_specs=(vmem,) * 5,
        scratch_shapes=[pltpu.VMEM(planes, f32)] * 2 + [pltpu.VMEM((kept, ring, side, ROWS, LANES), f32)],
        compiler_params=params,
        cost_estimate=pl.CostEstimate(flops=0, bytes_accessed=10**7, transcendentals=0),
    )(own, other, places, rates)
    odd_in, even_in, stepped = lax.optimization_barrier((odd_in, even_in, stepped))
    arrived = jnp.stack([even_in, odd_in])
    passed_on = lax.ppermute(arrived, AXES, owners)
    result, rim_around = pl.pallas_call(
        functools.partial(second_kernel, side, blocks, cores),
        out_shape=(
            jax.ShapeDtypeStruct((FIELDS, blocks, rows, LANES), f32),
            jax.ShapeDtypeStruct((kept, blocks, 2, ROWS, LANES), f32),
        ),
        in_specs=[vmem] * 5,
        out_specs=(vmem,) * 2,
        scratch_shapes=[
            pltpu.VMEM((4, FIELDS, blocks, side, ROWS, LANES), f32),
            pltpu.VMEM((kept, blocks, side, ROWS, LANES), f32),
        ],
        compiler_params=params,
        cost_estimate=pl.CostEstimate(flops=0, bytes_accessed=10**7, transcendentals=0),
    )(stepped, ups, downs, places, rates)
    results = pl.pallas_call(
        functools.partial(rim_kernel, side, blocks, cores, layers),
        out_shape=(jax.ShapeDtypeStruct((blocks, rows, LANES), f32),) * FIELDS,
        in_specs=[vmem] * 9,
        out_specs=(hbm,) * FIELDS,
        scratch_shapes=[
            pltpu.VMEM((2, FIELDS, ring, EDGE, ROWS, LANES), f32),
            pltpu.VMEM((2, FIELDS, ring, 2, ROWS, LANES), f32),
            pltpu.VMEM((3, 2, FIELDS, max(ring, 4 * blocks), ROWS, LANES), f32),
            pltpu.VMEM((kept, ring + blocks, 2, ROWS, LANES), f32),
            pltpu.VMEM((FIELDS, 2, blocks, ROWS * ROWS, LANES), f32),
            pltpu.SemaphoreType.DMA((FIELDS, 2)),
            pltpu.SemaphoreType.DMA((FIELDS,)),
        ],
        compiler_params=params,
        cost_estimate=pl.CostEstimate(flops=0, bytes_accessed=10**6, transcendentals=0),
    )(raw, stepped, result, face_around, rim_around, places, rates, arrived, passed_on)
    return tuple(block_of(r, side)[None] for r in results)


def solution(mesh):
    layers, cores = mesh.shape["slab"], mesh.shape["bal"]
    split, copied = P("slab", "bal", None, None), P()
    return jax.shard_map(
        functools.partial(body, layers, cores),
        mesh=mesh,
        in_specs=(split,) * 3 + (copied,) * 3,
        out_specs=(split,) * 3,
        check_vma=False,
    )
```

```python
import functools

import jax
import jax.numpy as jnp
from jax import lax
from jax.experimental import pallas as pl
from jax.experimental.pallas import tpu as pltpu
from jax.sharding import PartitionSpec as P

RATE = 0.1
ANISO = 0.05
COUPLE = 0.5
DIFF_SOLUTE = 0.08
DIFF_HEAT = 0.15
TINY = 0.0001
ROWS, LANES = 8, 128
EDGE = 2
FIELDS = 3
AXES = ("slab", "bal")
CHUNK_FIRST = 4
CROSSED = (1, 0)
SHIFTED_EARLY = 2
CHUNK_SECOND = 28
VMEM_BYTES = 40 * 2**20


def tiles_of(block):
    blocks, side, cells = block.shape
    split = block.reshape(blocks, side // ROWS, ROWS, cells // LANES, LANES)
    return split.transpose(0, 1, 3, 2, 4).reshape(blocks, side * cells // LANES, LANES)


def block_of(tiles, side):
    blocks, rows, _ = tiles.shape
    columns = rows // side
    split = tiles.reshape(blocks, side // ROWS, columns, ROWS, LANES)
    return split.transpose(0, 1, 3, 2, 4).reshape(blocks, side, columns * LANES)


def plane_rows(x):
    return pl.ds((x >> 3) * ROWS * ROWS + (x & (ROWS - 1)), ROWS, stride=ROWS)


def lane_ids():
    return lax.broadcasted_iota(jnp.int32, (ROWS, LANES), 1)


class Geometry:
    def __init__(self, side):
        lanes = lane_ids()
        self.side = side
        self.y_last = lanes >= LANES - side
        self.y_first = lanes < side
        self.z_first = lanes % side == 0
        self.z_last = lanes % side == side - 1

    def up(self, plane):
        return pltpu.roll(plane, LANES - self.side, 1)

    def down(self, plane):
        return pltpu.roll(plane, self.side, 1)

    def y_pair(self, up, down):
        upper = jnp.where(self.y_last, pltpu.roll(up, ROWS - 1, 0), up)
        lower = jnp.where(self.y_first, pltpu.roll(down, 1, 0), down)
        return upper, lower

    def z_pair(self, plane, next_down, previous_up):
        upper = pltpu.roll(jnp.where(self.z_first, next_down, plane), LANES - 1, 1)
        lower = pltpu.roll(jnp.where(self.z_last, previous_up, plane), 1, 1)
        return upper, lower


def advance(centers, sums, differences, rate):
    phase, solute, heat = centers
    sum_phase, sum_solute, sum_heat = sums
    squares = [d * d for d in differences]
    square = squares[0] + squares[1] + squares[2]
    quartic = squares[0] * squares[0] + squares[1] * squares[1] + squares[2] * squares[2]
    below = square * square + 16.0 * TINY
    anisotropy = (1.0 - 3.0 * ANISO) + 4.0 * ANISO * (quartic / below)
    well = 1.0 - phase * phase
    forcing = well * (phase - COUPLE * well * (solute + heat))
    change = rate * (anisotropy * anisotropy * (sum_phase - 6.0 * phase) + forcing)
    half = 0.5 * change
    return (
        phase + change,
        (1.0 - 6.0 * DIFF_SOLUTE) * solute + (DIFF_SOLUTE * sum_solute + half),
        (1.0 - 6.0 * DIFF_HEAT) * heat + (DIFF_HEAT * sum_heat + half),
    )


def sides(geometry, center, up, down, next_down, previous_up, phase):
    y_upper, y_lower = geometry.y_pair(up, down)
    z_upper, z_lower = geometry.z_pair(center, next_down, previous_up)
    total = (y_upper + y_lower) + (z_upper + z_lower)
    return (total, y_upper - y_lower, z_upper - z_lower) if phase else (total,)


def keep_sides(geometry, around, b, x, center, up, down, next_down, previous_up):
    for f in range(FIELDS):
        found = sides(geometry, center(f), up(f), down(f), next_down(f), previous_up(f), f == 0)
        for k, value in enumerate(found):
            around[f if k == 0 else FIELDS - 1 + k, b, x] = value


def finish(below, center, above, around, rate):
    sums = [(above[f] + below[f]) + around[f] for f in range(FIELDS)]
    return advance(center, sums, (above[0] - below[0], around[FIELDS], around[FIELDS + 1]), rate)


def planes_at(ref, p, x):
    return [ref[f, p, x] for f in range(FIELDS)]


def rate_of(active):
    return jnp.where(active != 0, jnp.float32(RATE), jnp.float32(0.0))


def start_tables(tables, held, sem):
    copies = [pltpu.make_async_copy(t, h, sem.at[i]) for i, (t, h) in enumerate(zip(tables, held))]
    for copy in copies:
        copy.start()
    return copies


def holders(before, layer, core, blocks, cores):
    found = [0] * (blocks * cores)
    for place in range(blocks * cores):
        owner = core if place < blocks else cores - 1 - core
        at = before[owner * blocks + place % blocks, layer]
        found = [jnp.where(at == p, place, found[p]) for p in range(len(found))]
    return found


def pack_kernel(side, blocks, cores, layers, *refs):
    fields, tables = refs[:FIELDS], refs[FIELDS : FIELDS + 3]
    even_ref, odd_ref, own, places_out, rates_out = refs[FIELDS + 3 : FIELDS + 8]
    before, after, flags, own_sem, table_sem = refs[FIELDS + 8 :]
    ring = blocks * cores
    layer, core = lax.axis_index("slab"), lax.axis_index("bal")
    own_copies = [pltpu.make_async_copy(fields[f], own.at[f], own_sem.at[f]) for f in range(FIELDS)]
    for copy in own_copies:
        copy.start()
    copies = start_tables(tables, (before, after, flags), table_sem)
    for copy in copies:
        copy.wait()
    beside = [jnp.clip(layer + 2 * end - 1, 0, layers - 1) for end in range(2)]
    listed = holders(before, layer, core, blocks, cores)
    listed += [after[core * blocks + b, layer] for b in range(blocks)]
    for end, table in enumerate(beside):
        crossed = jnp.where(lax.rem(layer, 2) == 1 - end, *CROSSED)
        sender = jnp.where(crossed == 1, cores - 1 - core, core)
        for c in range(cores):
            slot = (sender if c == 0 else cores - 1 - sender) * blocks
            listed += [before[slot + b, table] for b in range(blocks)]
    for k, place in enumerate(listed):
        places_out[k] = jnp.full((ROWS, LANES), place, jnp.int32)
    rates = [rate_of(flags[p, table]) for table in [layer] + beside for p in range(ring)]
    for k, rate in enumerate(rates):
        rates_out[k] = jnp.full((ROWS, LANES), rate, jnp.float32)
    is_even = lax.rem(layer, 2) == 0
    for f in range(FIELDS):
        own_copies[f].wait()
        for b in range(blocks):
            for d in range(EDGE):
                lower, upper = own[f, b, plane_rows(d)], own[f, b, plane_rows(side - 1 - d)]
                even_ref[f, b, d] = jnp.where(is_even, upper, lower)
                odd_ref[f, b, d] = jnp.where(is_even, lower, upper)


def spread(geometry, planes, sources, raw, ups, downs):
    for x in planes:
        for f in range(FIELDS):
            for place, source in sources.items():
                for b in range(source.shape[1]):
                    plane = source[f, b, plane_rows(x)]
                    raw[f, place + b, x] = plane
                    ups[f, place + b, x] = geometry.up(plane)
                    downs[f, place + b, x] = geometry.down(plane)


def early_kernel(side, own, raw, ups, downs):
    @pl.when(lax.axis_index("slab") == 0)
    def _():
        spread(Geometry(side), range(side), {0: own}, raw, ups, downs)


def first_kernel(side, blocks, cores, *refs):
    own, other, places_ref, rates_ref = refs[:4]
    raw, ups, downs, stepped, next_ups, next_downs, face_around, around = refs[7:]
    ring = blocks * cores
    geometry = Geometry(side)
    places = [place_at(places_ref, p) for p in range(ring)]
    rates = [rates_ref[p] for p in range(ring)]

    def gather(planes):
        for x in planes:
            face = x in (0, side - 1)
            for p in range(ring):
                here, following, previous = places[p], places[(p + 1) % ring], places[(p - 1) % ring]
                keep_sides(
                    geometry,
                    face_around if face else around,
                    p,
                    x // (side - 1) if face else x,
                    lambda f: raw[f, here, x],
                    lambda f: ups[f, here, x],
                    lambda f: downs[f, here, x],
                    lambda f: downs[f, following, x],
                    lambda f: ups[f, previous, x],
                )

    def calculate(planes):
        for x in planes:
            for p in range(ring):
                low, center, high = (planes_at(raw, places[p], x + d) for d in (-1, 0, 1))
                new = finish(low, center, high, [around[k, p, x] for k in range(FIELDS + 2)], rates[p])
                for f in range(FIELDS):
                    stepped[f, p, x] = new[f]
                    if f < SHIFTED_EARLY:
                        next_ups[f, p, x] = geometry.up(new[f])
                        next_downs[f, p, x] = geometry.down(new[f])

    def steps(sources):
        count = side // CHUNK_FIRST
        spread(geometry, range(CHUNK_FIRST), sources, raw, ups, downs)
        for c in range(count):
            planes = range(c * CHUNK_FIRST, (c + 1) * CHUNK_FIRST)
            gather(planes)
            if c + 1 < count:
                spread(geometry, [x + CHUNK_FIRST for x in planes], sources, raw, ups, downs)
            calculate([x for x in planes if 0 < x < side - 1])

    is_early = lax.axis_index("slab") == 0
    pl.when(is_early)(lambda: steps({blocks: other}))
    pl.when(jnp.logical_not(is_early))(lambda: steps({0: own, blocks: other}))


def place_at(ref, k):
    return ref[k][0, 0]


def second_kernel(side, blocks, cores, *refs):
    stepped, ups, downs, places_ref, rates_ref, result, rim_around, shifted, around = refs
    ring = blocks * cores
    geometry = Geometry(side)
    places = [place_at(places_ref, ring + b) for b in range(blocks)]
    rates = [rates_ref[p] for p in places]

    rounds = [(p, (p + 1) & (ring - 1), (p + ring - 1) & (ring - 1)) for p in places]

    def shift(x):
        for b, (p, following, previous) in enumerate(rounds):
            for f in range(SHIFTED_EARLY, FIELDS):
                shifted[0, f, b, x] = geometry.up(stepped[f, p, x])
                shifted[1, f, b, x] = geometry.down(stepped[f, p, x])
                shifted[2, f, b, x] = geometry.down(stepped[f, following, x])
                shifted[3, f, b, x] = geometry.up(stepped[f, previous, x])

    def gather(x, target, at):
        for b, (p, following, previous) in enumerate(rounds):
            keep_sides(
                geometry,
                target,
                b,
                at,
                lambda f: stepped[f, p, x],
                lambda f: ups[f, p, x] if f < SHIFTED_EARLY else shifted[0, f, b, x],
                lambda f: downs[f, p, x] if f < SHIFTED_EARLY else shifted[1, f, b, x],
                lambda f: downs[f, following, x] if f < SHIFTED_EARLY else shifted[2, f, b, x],
                lambda f: ups[f, previous, x] if f < SHIFTED_EARLY else shifted[3, f, b, x],
            )

    @pl.loop(0, (side - 4) // CHUNK_SECOND)
    def _(i):
        planes = [2 + i * CHUNK_SECOND + u for u in range(CHUNK_SECOND)]
        for x in planes:
            shift(x)
        for x in planes:
            gather(x, around, x)
        for x in planes:
            for b, p in enumerate(places):
                low, center, high = (planes_at(stepped, p, x + d) for d in (-1, 0, 1))
                new = finish(low, center, high, [around[k, b, x] for k in range(FIELDS + 2)], rates[b])
                for f in range(FIELDS):
                    result[f, b, plane_rows(x)] = new[f]

    for end in range(2):
        shift(1 + end * (side - 3))
    for end in range(2):
        gather(1 + end * (side - 3), rim_around, end)


def rim_kernel(side, blocks, cores, layers, *refs):
    raw, inner, result, face_around, rim_around, places_ref, rates_ref = refs[:7]
    messages = refs[7:9]
    outs = refs[9 : 9 + FIELDS]
    halo, faces, shifted, around, tiles, sem, middle_sem = refs[9 + FIELDS :]
    ring = blocks * cores
    layer = lax.axis_index("slab")
    parity = lax.rem(layer, 2)
    geometry = Geometry(side)
    rows = ROWS * ROWS
    middle = pl.ds(rows, side * ROWS - 2 * rows)
    copies = [
        pltpu.make_async_copy(result.at[f, :, middle], outs[f].at[:, middle], middle_sem.at[f])
        for f in range(FIELDS)
    ]
    for copy in copies:
        copy.start()
    places = [place_at(places_ref, p) for p in range(ring)]
    targets = [place_at(places_ref, ring + b) for b in range(blocks)]
    beside = [layer + 2 * end - 1 for end in range(2)]
    outside = [jnp.logical_or(b < 0, b >= layers) for b in beside]
    ends = range(2)

    def at_face(end, p, d):
        return planes_at(raw, places[p], d if end == 0 else side - 1 - d)

    for end in ends:
        message = jnp.where(parity == 1 - end, 0, 1)
        for c in range(cores):
            for b in range(blocks):
                p = place_at(places_ref, ring + blocks + (end * cores + c) * blocks + b)
                for f in range(FIELDS):
                    for d in range(EDGE):
                        halo[end, f, p, d] = messages[c][message, f, b, d]
    for f in range(FIELDS):
        for end in ends:
            tiles[f, end] = result[f, :, pl.ds(end * (side * ROWS - rows), rows)]
    for end in ends:
        for p in range(ring):
            for f in range(FIELDS):
                near = jnp.where(outside[end], at_face(end, p, 0)[f], halo[end, f, p, 0])
                halo[end, f, p, 0] = near
                shifted[0, end, f, p] = geometry.up(near)
                shifted[1, end, f, p] = geometry.down(near)
    for end in ends:
        for p in range(ring):
            new = finish(
                [halo[end, f, p, 0] for f in range(FIELDS)],
                at_face(end, p, 0),
                at_face(end, p, 1),
                [face_around[k, p, end] for k in range(FIELDS + 2)],
                rates_ref[p],
            )
            for f in range(FIELDS):
                faces[end, f, p, 1] = new[f]
    for end in ends:
        for p in range(ring):
            keep_sides(
                geometry,
                around,
                p,
                end,
                lambda f: halo[end, f, p, 0],
                lambda f: shifted[0, end, f, p],
                lambda f: shifted[1, end, f, p],
                lambda f: shifted[1, end, f, (p + 1) % ring],
                lambda f: shifted[0, end, f, (p - 1) % ring],
            )
    rounds = [(p, (p + 1) & (ring - 1), (p + ring - 1) & (ring - 1)) for p in targets]
    for end in ends:
        for b, (p, following, previous) in enumerate(rounds):
            for f in range(FIELDS):
                shifted[2, end, f, 4 * b] = geometry.up(faces[end, f, p, 1])
                shifted[2, end, f, 4 * b + 1] = geometry.down(faces[end, f, p, 1])
                shifted[2, end, f, 4 * b + 2] = geometry.down(faces[end, f, following, 1])
                shifted[2, end, f, 4 * b + 3] = geometry.up(faces[end, f, previous, 1])
    for end in ends:
        for p in range(ring):
            new = finish(
                [halo[end, f, p, 1] for f in range(FIELDS)],
                [halo[end, f, p, 0] for f in range(FIELDS)],
                at_face(end, p, 0),
                [around[k, p, end] for k in range(FIELDS + 2)],
                rates_ref[ring * (1 + end) + p],
            )
            for f in range(FIELDS):
                faces[end, f, p, 0] = jnp.where(outside[end], faces[end, f, p, 1], new[f])
    for end in ends:
        for b, (p, following, previous) in enumerate(rounds):
            keep_sides(
                geometry,
                around,
                ring + b,
                end,
                lambda f: faces[end, f, p, 1],
                lambda f: shifted[2, end, f, 4 * b],
                lambda f: shifted[2, end, f, 4 * b + 1],
                lambda f: shifted[2, end, f, 4 * b + 2],
                lambda f: shifted[2, end, f, 4 * b + 3],
            )
    for end in ends:
        for b, p in enumerate(targets):
            outer, face = ([faces[end, f, p, d] for f in range(FIELDS)] for d in range(2))
            first, second = (planes_at(inner, p, d if end == 0 else side - 1 - d) for d in (1, 2))
            news = (
                finish(outer, face, first, [around[k, ring + b, end] for k in range(FIELDS + 2)], rates_ref[p]),
                finish(face, first, second, [rim_around[k, b, end] for k in range(FIELDS + 2)], rates_ref[p]),
            )
            for d in range(EDGE):
                row = d if end == 0 else ROWS - 1 - d
                for f in range(FIELDS):
                    tiles[f, end, b, pl.ds(row, ROWS, stride=ROWS)] = news[d][f]
        for f in range(FIELDS):
            part = pl.ds(end * (side * ROWS - rows), rows)
            copies.append(pltpu.make_async_copy(tiles.at[f, end], outs[f].at[:, part], sem.at[f, end]))
            copies[-1].start()
    for copy in copies:
        copy.wait()


def neighbour_swaps(layers, cores, first):
    pairs = []
    for layer in range(layers):
        partner = layer + 1 if (layer - first) % 2 == 0 else layer - 1
        for core in range(cores):
            here = layer * cores + core
            if 0 <= partner < layers:
                pairs.append((here, partner * cores + (cores - 1 - core if CROSSED[first] else core)))
            else:
                pairs.append((here, layer * cores + cores - 1 - core))
    return pairs


def body(layers, cores, order_parameter, concentration_excess, thermal_subcooling, before, after, flags):
    blocks, side = order_parameter.shape[1], order_parameter.shape[2]
    ring = blocks * cores
    rows = side * ROWS
    f32 = jnp.float32
    before, after, flags = before.T, after.T, flags.T
    owners = [(s * cores + c, s * cores + cores - 1 - c) for s in range(layers) for c in range(cores)]
    fields = [tiles_of(a[0]) for a in (order_parameter, concentration_excess, thermal_subcooling)]
    vmem, hbm = (pl.BlockSpec(memory_space=m) for m in (pltpu.VMEM, pltpu.HBM))
    params = pltpu.CompilerParams(vmem_limit_bytes=VMEM_BYTES)
    message = jax.ShapeDtypeStruct((FIELDS, blocks, EDGE, ROWS, LANES), f32)
    table = pltpu.SMEM(before.shape, jnp.int32)
    in_hbm = lambda *arrays: [pltpu.with_memory_space_constraint(a, pltpu.HBM) for a in arrays]
    numbers = (
        jax.ShapeDtypeStruct((3 * ring + blocks, ROWS, LANES), jnp.int32),
        jax.ShapeDtypeStruct((3 * ring, ROWS, LANES), f32),
    )
    even, odd, own, places, rates = pl.pallas_call(
        functools.partial(pack_kernel, side, blocks, cores, layers),
        out_shape=(message, message, jax.ShapeDtypeStruct((FIELDS, blocks, rows, LANES), f32)) + numbers,
        in_specs=[hbm] * (FIELDS + 3),
        out_specs=(vmem,) * 5,
        scratch_shapes=[table] * 3
        + [pltpu.SemaphoreType.DMA((FIELDS,)), pltpu.SemaphoreType.DMA((3,))],
        compiler_params=params,
        cost_estimate=pl.CostEstimate(flops=0, bytes_accessed=10**6, transcendentals=0),
    )(*in_hbm(*fields, before, after, flags))
    other = lax.ppermute(own, AXES, owners)
    odd_in = lax.ppermute(odd, AXES, neighbour_swaps(layers, cores, 1))
    planes = (FIELDS, ring, side, ROWS, LANES)
    kept = FIELDS + 2
    three = (jax.ShapeDtypeStruct(planes, f32),) * 3
    early = pl.pallas_call(
        functools.partial(early_kernel, side),
        out_shape=three,
        in_specs=[vmem],
        out_specs=(vmem,) * 3,
        compiler_params=params,
        cost_estimate=pl.CostEstimate(flops=0, bytes_accessed=10**6, transcendentals=0),
    )(own)
    even, *early = lax.optimization_barrier((even, *early))
    even_in = lax.ppermute(even, AXES, neighbour_swaps(layers, cores, 0))
    raw, _, _, stepped, ups, downs, face_around = pl.pallas_call(
        functools.partial(first_kernel, side, blocks, cores),
        out_shape=three * 2 + (jax.ShapeDtypeStruct((kept, ring, 2, ROWS, LANES), f32),),
        in_specs=[vmem] * 7,
        out_specs=(vmem,) * 7,
        input_output_aliases={4 + k: k for k in range(3)},
        scratch_shapes=[pltpu.VMEM((kept, ring, side, ROWS, LANES), f32)],
        compiler_params=params,
        cost_estimate=pl.CostEstimate(flops=0, bytes_accessed=10**7, transcendentals=0),
    )(own, other, places, rates, *early)
    odd_in, even_in, stepped = lax.optimization_barrier((odd_in, even_in, stepped))
    arrived = jnp.stack([even_in, odd_in])
    passed_on = lax.ppermute(arrived, AXES, owners)
    result, rim_around = pl.pallas_call(
        functools.partial(second_kernel, side, blocks, cores),
        out_shape=(
            jax.ShapeDtypeStruct((FIELDS, blocks, rows, LANES), f32),
            jax.ShapeDtypeStruct((kept, blocks, 2, ROWS, LANES), f32),
        ),
        in_specs=[vmem] * 5,
        out_specs=(vmem,) * 2,
        scratch_shapes=[
            pltpu.VMEM((4, FIELDS, blocks, side, ROWS, LANES), f32),
            pltpu.VMEM((kept, blocks, side, ROWS, LANES), f32),
        ],
        compiler_params=params,
        cost_estimate=pl.CostEstimate(flops=0, bytes_accessed=10**7, transcendentals=0),
    )(stepped, ups, downs, places, rates)
    results = pl.pallas_call(
        functools.partial(rim_kernel, side, blocks, cores, layers),
        out_shape=(jax.ShapeDtypeStruct((blocks, rows, LANES), f32),) * FIELDS,
        in_specs=[vmem] * 9,
        out_specs=(hbm,) * FIELDS,
        scratch_shapes=[
            pltpu.VMEM((2, FIELDS, ring, EDGE, ROWS, LANES), f32),
            pltpu.VMEM((2, FIELDS, ring, 2, ROWS, LANES), f32),
            pltpu.VMEM((3, 2, FIELDS, max(ring, 4 * blocks), ROWS, LANES), f32),
            pltpu.VMEM((kept, ring + blocks, 2, ROWS, LANES), f32),
            pltpu.VMEM((FIELDS, 2, blocks, ROWS * ROWS, LANES), f32),
            pltpu.SemaphoreType.DMA((FIELDS, 2)),
            pltpu.SemaphoreType.DMA((FIELDS,)),
        ],
        compiler_params=params,
        cost_estimate=pl.CostEstimate(flops=0, bytes_accessed=10**6, transcendentals=0),
    )(raw, stepped, result, face_around, rim_around, places, rates, arrived, passed_on)
    return tuple(block_of(r, side)[None] for r in results)


def solution(mesh):
    layers, cores = mesh.shape["slab"], mesh.shape["bal"]
    split, copied = P("slab", "bal", None, None), P()
    return jax.shard_map(
        functools.partial(body, layers, cores),
        mesh=mesh,
        in_specs=(split,) * 3 + (copied,) * 3,
        out_specs=(split,) * 3,
        check_vma=False,
    )
```

```python
import functools

import jax
import jax.numpy as jnp
from jax import lax
from jax.experimental import pallas as pl
from jax.experimental.pallas import tpu as pltpu
from jax.sharding import PartitionSpec as P

RATE = 0.1
ANISO = 0.05
COUPLE = 0.5
DIFF_SOLUTE = 0.08
DIFF_HEAT = 0.15
TINY = 0.0001
ROWS, LANES = 8, 128
EDGE = 2
FIELDS = 3
AXES = ("slab", "bal")
CHUNK_FIRST = 4
CROSSED = (1, 0)
SHIFTED_EARLY = 3
CHUNK_SECOND = 28
VMEM_BYTES = 40 * 2**20


def tiles_of(block):
    blocks, side, cells = block.shape
    split = block.reshape(blocks, side // ROWS, ROWS, cells // LANES, LANES)
    return split.transpose(0, 1, 3, 2, 4).reshape(blocks, side * cells // LANES, LANES)


def block_of(tiles, side):
    blocks, rows, _ = tiles.shape
    columns = rows // side
    split = tiles.reshape(blocks, side // ROWS, columns, ROWS, LANES)
    return split.transpose(0, 1, 3, 2, 4).reshape(blocks, side, columns * LANES)


def plane_rows(x):
    return pl.ds((x >> 3) * ROWS * ROWS + (x & (ROWS - 1)), ROWS, stride=ROWS)


def lane_ids():
    return lax.broadcasted_iota(jnp.int32, (ROWS, LANES), 1)


class Geometry:
    def __init__(self, side):
        lanes = lane_ids()
        self.side = side
        self.y_last = lanes >= LANES - side
        self.y_first = lanes < side
        self.z_first = lanes % side == 0
        self.z_last = lanes % side == side - 1

    def up(self, plane):
        return pltpu.roll(plane, LANES - self.side, 1)

    def down(self, plane):
        return pltpu.roll(plane, self.side, 1)

    def y_pair(self, up, down):
        upper = jnp.where(self.y_last, pltpu.roll(up, ROWS - 1, 0), up)
        lower = jnp.where(self.y_first, pltpu.roll(down, 1, 0), down)
        return upper, lower

    def z_pair(self, plane, next_down, previous_up):
        upper = pltpu.roll(jnp.where(self.z_first, next_down, plane), LANES - 1, 1)
        lower = pltpu.roll(jnp.where(self.z_last, previous_up, plane), 1, 1)
        return upper, lower


def advance(centers, sums, differences, rate):
    phase, solute, heat = centers
    sum_phase, sum_solute, sum_heat = sums
    squares = [d * d for d in differences]
    square = squares[0] + squares[1] + squares[2]
    quartic = squares[0] * squares[0] + squares[1] * squares[1] + squares[2] * squares[2]
    below = square * square + 16.0 * TINY
    anisotropy = (1.0 - 3.0 * ANISO) + 4.0 * ANISO * (quartic / below)
    well = 1.0 - phase * phase
    forcing = well * (phase - COUPLE * well * (solute + heat))
    change = rate * (anisotropy * anisotropy * (sum_phase - 6.0 * phase) + forcing)
    half = 0.5 * change
    return (
        phase + change,
        (1.0 - 6.0 * DIFF_SOLUTE) * solute + (DIFF_SOLUTE * sum_solute + half),
        (1.0 - 6.0 * DIFF_HEAT) * heat + (DIFF_HEAT * sum_heat + half),
    )


def sides(geometry, center, up, down, next_down, previous_up, phase):
    y_upper, y_lower = geometry.y_pair(up, down)
    z_upper, z_lower = geometry.z_pair(center, next_down, previous_up)
    total = (y_upper + y_lower) + (z_upper + z_lower)
    return (total, y_upper - y_lower, z_upper - z_lower) if phase else (total,)


def keep_sides(geometry, around, b, x, center, up, down, next_down, previous_up):
    for f in range(FIELDS):
        found = sides(geometry, center(f), up(f), down(f), next_down(f), previous_up(f), f == 0)
        for k, value in enumerate(found):
            around[f if k == 0 else FIELDS - 1 + k, b, x] = value


def finish(below, center, above, around, rate):
    sums = [(above[f] + below[f]) + around[f] for f in range(FIELDS)]
    return advance(center, sums, (above[0] - below[0], around[FIELDS], around[FIELDS + 1]), rate)


def planes_at(ref, p, x):
    return [ref[f, p, x] for f in range(FIELDS)]


def rate_of(active):
    return jnp.where(active != 0, jnp.float32(RATE), jnp.float32(0.0))


def start_tables(tables, held, sem):
    copies = [pltpu.make_async_copy(t, h, sem.at[i]) for i, (t, h) in enumerate(zip(tables, held))]
    for copy in copies:
        copy.start()
    return copies


def holders(before, layer, core, blocks, cores):
    found = [0] * (blocks * cores)
    for place in range(blocks * cores):
        owner = core if place < blocks else cores - 1 - core
        at = before[owner * blocks + place % blocks, layer]
        found = [jnp.where(at == p, place, found[p]) for p in range(len(found))]
    return found


def pack_kernel(side, blocks, cores, layers, *refs):
    fields, tables = refs[:FIELDS], refs[FIELDS : FIELDS + 3]
    even_ref, odd_ref, own, places_out, rates_out = refs[FIELDS + 3 : FIELDS + 8]
    before, after, flags, own_sem, table_sem = refs[FIELDS + 8 :]
    ring = blocks * cores
    layer, core = lax.axis_index("slab"), lax.axis_index("bal")
    own_copies = [pltpu.make_async_copy(fields[f], own.at[f], own_sem.at[f]) for f in range(FIELDS)]
    for copy in own_copies:
        copy.start()
    copies = start_tables(tables, (before, after, flags), table_sem)
    for copy in copies:
        copy.wait()
    beside = [jnp.clip(layer + 2 * end - 1, 0, layers - 1) for end in range(2)]
    listed = holders(before, layer, core, blocks, cores)
    listed += [after[core * blocks + b, layer] for b in range(blocks)]
    for end, table in enumerate(beside):
        crossed = jnp.where(lax.rem(layer, 2) == 1 - end, *CROSSED)
        sender = jnp.where(crossed == 1, cores - 1 - core, core)
        for c in range(cores):
            slot = (sender if c == 0 else cores - 1 - sender) * blocks
            listed += [before[slot + b, table] for b in range(blocks)]
    for k, place in enumerate(listed):
        places_out[k] = jnp.full((ROWS, LANES), place, jnp.int32)
    rates = [rate_of(flags[p, table]) for table in [layer] + beside for p in range(ring)]
    for k, rate in enumerate(rates):
        rates_out[k] = jnp.full((ROWS, LANES), rate, jnp.float32)
    is_even = lax.rem(layer, 2) == 0
    for f in range(FIELDS):
        own_copies[f].wait()
        for b in range(blocks):
            for d in range(EDGE):
                lower, upper = own[f, b, plane_rows(d)], own[f, b, plane_rows(side - 1 - d)]
                even_ref[f, b, d] = jnp.where(is_even, upper, lower)
                odd_ref[f, b, d] = jnp.where(is_even, lower, upper)


def spread(geometry, planes, sources, raw, ups, downs):
    for x in planes:
        for f in range(FIELDS):
            for place, source in sources.items():
                for b in range(source.shape[1]):
                    plane = source[f, b, plane_rows(x)]
                    raw[f, place + b, x] = plane
                    ups[f, place + b, x] = geometry.up(plane)
                    downs[f, place + b, x] = geometry.down(plane)


def early_kernel(side, own, raw, ups, downs):
    @pl.when(lax.axis_index("slab") == 0)
    def _():
        spread(Geometry(side), range(side), {0: own}, raw, ups, downs)


def first_kernel(side, blocks, cores, *refs):
    own, other, places_ref, rates_ref = refs[:4]
    raw, ups, downs, stepped, next_ups, next_downs, face_around, around = refs[7:]
    ring = blocks * cores
    geometry = Geometry(side)
    places = [place_at(places_ref, p) for p in range(ring)]
    rates = [rates_ref[p] for p in range(ring)]

    def gather(planes):
        for x in planes:
            face = x in (0, side - 1)
            for p in range(ring):
                here, following, previous = places[p], places[(p + 1) % ring], places[(p - 1) % ring]
                keep_sides(
                    geometry,
                    face_around if face else around,
                    p,
                    x // (side - 1) if face else x,
                    lambda f: raw[f, here, x],
                    lambda f: ups[f, here, x],
                    lambda f: downs[f, here, x],
                    lambda f: downs[f, following, x],
                    lambda f: ups[f, previous, x],
                )

    def calculate(planes):
        for x in planes:
            for p in range(ring):
                low, center, high = (planes_at(raw, places[p], x + d) for d in (-1, 0, 1))
                new = finish(low, center, high, [around[k, p, x] for k in range(FIELDS + 2)], rates[p])
                for f in range(FIELDS):
                    stepped[f, p, x] = new[f]
                    if f < SHIFTED_EARLY:
                        next_ups[f, p, x] = geometry.up(new[f])
                        next_downs[f, p, x] = geometry.down(new[f])

    def steps(sources):
        count = side // CHUNK_FIRST
        spread(geometry, range(CHUNK_FIRST), sources, raw, ups, downs)
        for c in range(count):
            planes = range(c * CHUNK_FIRST, (c + 1) * CHUNK_FIRST)
            gather(planes)
            if c + 1 < count:
                spread(geometry, [x + CHUNK_FIRST for x in planes], sources, raw, ups, downs)
            calculate([x for x in planes if 0 < x < side - 1])

    is_early = lax.axis_index("slab") == 0
    pl.when(is_early)(lambda: steps({blocks: other}))
    pl.when(jnp.logical_not(is_early))(lambda: steps({0: own, blocks: other}))


def place_at(ref, k):
    return ref[k][0, 0]


def second_kernel(side, blocks, cores, layers, *refs):
    stepped, ups, downs, places_ref, rates_ref, raw, face_around = refs[:7]
    result, rim_around, shifted, around, faces = refs[7:]
    ring = blocks * cores
    geometry = Geometry(side)
    places = [place_at(places_ref, ring + b) for b in range(blocks)]
    rates = [rates_ref[p] for p in places]

    rounds = [(p, (p + 1) & (ring - 1), (p + ring - 1) & (ring - 1)) for p in places]

    def shift(x):
        for b, (p, following, previous) in enumerate(rounds):
            for f in range(SHIFTED_EARLY, FIELDS):
                shifted[0, f, b, x] = geometry.up(stepped[f, p, x])
                shifted[1, f, b, x] = geometry.down(stepped[f, p, x])
                shifted[2, f, b, x] = geometry.down(stepped[f, following, x])
                shifted[3, f, b, x] = geometry.up(stepped[f, previous, x])

    def gather(x, target, at):
        for b, (p, following, previous) in enumerate(rounds):
            keep_sides(
                geometry,
                target,
                b,
                at,
                lambda f: stepped[f, p, x],
                lambda f: ups[f, p, x] if f < SHIFTED_EARLY else shifted[0, f, b, x],
                lambda f: downs[f, p, x] if f < SHIFTED_EARLY else shifted[1, f, b, x],
                lambda f: downs[f, following, x] if f < SHIFTED_EARLY else shifted[2, f, b, x],
                lambda f: ups[f, previous, x] if f < SHIFTED_EARLY else shifted[3, f, b, x],
            )

    @pl.loop(0, (side - 4) // CHUNK_SECOND)
    def _(i):
        planes = [2 + i * CHUNK_SECOND + u for u in range(CHUNK_SECOND)]
        for x in planes:
            shift(x)
        for x in planes:
            gather(x, around, x)
        for x in planes:
            for b, p in enumerate(places):
                low, center, high = (planes_at(stepped, p, x + d) for d in (-1, 0, 1))
                new = finish(low, center, high, [around[k, b, x] for k in range(FIELDS + 2)], rates[b])
                for f in range(FIELDS):
                    result[f, b, plane_rows(x)] = new[f]

    for end in range(2):
        shift(1 + end * (side - 3))
    for end in range(2):
        gather(1 + end * (side - 3), rim_around, end)


    layer = lax.axis_index("slab")

    def close(end):
        x = [d if end == 0 else side - 1 - d for d in range(3)]
        for p in range(ring):
            place = place_at(places_ref, p)
            near = planes_at(raw, place, x[0])
            new = finish(
                near, near, planes_at(raw, place, x[1]), [face_around[k, p, end] for k in range(FIELDS + 2)], rates_ref[p]
            )
            for f in range(FIELDS):
                faces[f, p] = new[f]
        for b, (p, following, previous) in enumerate(rounds):
            for f in range(FIELDS):
                shifted[0, f, b, x[0]] = geometry.up(faces[f, p])
                shifted[1, f, b, x[0]] = geometry.down(faces[f, p])
                shifted[2, f, b, x[0]] = geometry.down(faces[f, following])
                shifted[3, f, b, x[0]] = geometry.up(faces[f, previous])
        for b, p in enumerate(places):
            keep_sides(
                geometry,
                around,
                b,
                x[0],
                lambda f: faces[f, p],
                lambda f: shifted[0, f, b, x[0]],
                lambda f: shifted[1, f, b, x[0]],
                lambda f: shifted[2, f, b, x[0]],
                lambda f: shifted[3, f, b, x[0]],
            )
        for b, p in enumerate(places):
            face = [faces[f, p] for f in range(FIELDS)]
            first, second = planes_at(stepped, p, x[1]), planes_at(stepped, p, x[2])
            news = (
                finish(face, face, first, [around[k, b, x[0]] for k in range(FIELDS + 2)], rates[b]),
                finish(face, first, second, [rim_around[k, b, end] for k in range(FIELDS + 2)], rates[b]),
            )
            for d in range(EDGE):
                for f in range(FIELDS):
                    result[f, b, plane_rows(x[d])] = news[d][f]

    pl.when(layer == 0)(lambda: close(0))
    pl.when(layer == layers - 1)(lambda: close(1))


def rim_kernel(side, blocks, cores, layers, *refs):
    raw, inner, result, face_around, rim_around, places_ref, rates_ref = refs[:7]
    messages = refs[7:9]
    outs = refs[9 : 9 + FIELDS]
    halo, faces, shifted, around, tiles, sem, middle_sem = refs[9 + FIELDS :]
    ring = blocks * cores
    layer = lax.axis_index("slab")
    parity = lax.rem(layer, 2)
    geometry = Geometry(side)
    rows = ROWS * ROWS
    middle = pl.ds(rows, side * ROWS - 2 * rows)
    copies = [
        pltpu.make_async_copy(result.at[f, :, middle], outs[f].at[:, middle], middle_sem.at[f])
        for f in range(FIELDS)
    ]
    for copy in copies:
        copy.start()
    places = [place_at(places_ref, p) for p in range(ring)]
    targets = [place_at(places_ref, ring + b) for b in range(blocks)]
    rounds = [(p, (p + 1) & (ring - 1), (p + ring - 1) & (ring - 1)) for p in targets]

    def end_rows(end):
        return pl.ds(end * (side * ROWS - rows) if isinstance(end, int) else pl.multiple_of(end * (side * ROWS - rows), rows), rows)


    def rim(ends, done):
        out_copies = [pltpu.make_async_copy(result.at[f, :, end_rows(end)], outs[f].at[:, end_rows(end)], sem.at[f, end]) for end in done for f in range(FIELDS)]
        for copy in out_copies:
            copy.start()

        def outside(end):
            beside = layer + 2 * end - 1
            return jnp.logical_or(beside < 0, beside >= layers)

        def at_face(end, p, d):
            return planes_at(raw, places[p], d + end * (side - 1 - 2 * d))

        for end in ends:
            message = jnp.where(parity == 1 - end, 0, 1)
            for c in range(cores):
                for b in range(blocks):
                    p = place_at(places_ref, ring + blocks + (end * cores + c) * blocks + b)
                    for f in range(FIELDS):
                        for d in range(EDGE):
                            halo[end, f, p, d] = messages[c][message, f, b, d]
        for f in range(FIELDS):
            for end in ends:
                tiles[f, end] = result[f, :, end_rows(end)]
        for end in ends:
            for p in range(ring):
                for f in range(FIELDS):
                    near = jnp.where(outside(end), at_face(end, p, 0)[f], halo[end, f, p, 0])
                    halo[end, f, p, 0] = near
                    shifted[0, end, f, p] = geometry.up(near)
                    shifted[1, end, f, p] = geometry.down(near)
        for end in ends:
            for p in range(ring):
                new = finish(
                    [halo[end, f, p, 0] for f in range(FIELDS)],
                    at_face(end, p, 0),
                    at_face(end, p, 1),
                    [face_around[k, p, end] for k in range(FIELDS + 2)],
                    rates_ref[p],
                )
                for f in range(FIELDS):
                    faces[end, f, p, 1] = new[f]
        for end in ends:
            for p in range(ring):
                keep_sides(
                    geometry,
                    around,
                    p,
                    end,
                    lambda f: halo[end, f, p, 0],
                    lambda f: shifted[0, end, f, p],
                    lambda f: shifted[1, end, f, p],
                    lambda f: shifted[1, end, f, (p + 1) % ring],
                    lambda f: shifted[0, end, f, (p - 1) % ring],
                )
        for end in ends:
            for b, (p, following, previous) in enumerate(rounds):
                for f in range(FIELDS):
                    shifted[2, end, f, 4 * b] = geometry.up(faces[end, f, p, 1])
                    shifted[2, end, f, 4 * b + 1] = geometry.down(faces[end, f, p, 1])
                    shifted[2, end, f, 4 * b + 2] = geometry.down(faces[end, f, following, 1])
                    shifted[2, end, f, 4 * b + 3] = geometry.up(faces[end, f, previous, 1])
        for end in ends:
            for p in range(ring):
                new = finish(
                    [halo[end, f, p, 1] for f in range(FIELDS)],
                    [halo[end, f, p, 0] for f in range(FIELDS)],
                    at_face(end, p, 0),
                    [around[k, p, end] for k in range(FIELDS + 2)],
                    rates_ref[ring * (1 + end) + p],
                )
                for f in range(FIELDS):
                    faces[end, f, p, 0] = jnp.where(outside(end), faces[end, f, p, 1], new[f])
        for end in ends:
            for b, (p, following, previous) in enumerate(rounds):
                keep_sides(
                    geometry,
                    around,
                    ring + b,
                    end,
                    lambda f: faces[end, f, p, 1],
                    lambda f: shifted[2, end, f, 4 * b],
                    lambda f: shifted[2, end, f, 4 * b + 1],
                    lambda f: shifted[2, end, f, 4 * b + 2],
                    lambda f: shifted[2, end, f, 4 * b + 3],
                )
        for end in ends:
            for b, p in enumerate(targets):
                outer, face = ([faces[end, f, p, d] for f in range(FIELDS)] for d in range(2))
                first, second = (planes_at(inner, p, d + end * (side - 1 - 2 * d)) for d in (1, 2))
                news = (
                    finish(outer, face, first, [around[k, ring + b, end] for k in range(FIELDS + 2)], rates_ref[p]),
                    finish(face, first, second, [rim_around[k, b, end] for k in range(FIELDS + 2)], rates_ref[p]),
                )
                for d in range(EDGE):
                    row = d + end * (ROWS - 1 - 2 * d)
                    for f in range(FIELDS):
                        tiles[f, end, b, pl.ds(row, ROWS, stride=ROWS)] = news[d][f]
            for f in range(FIELDS):
                part = end_rows(end)
                out_copies.append(pltpu.make_async_copy(tiles.at[f, end], outs[f].at[:, part], sem.at[f, end]))
                out_copies[-1].start()
        for copy in out_copies:
            copy.wait()

    is_lowest, is_highest = layer == 0, layer == layers - 1
    at_edge = jnp.logical_or(is_lowest, is_highest)
    open_end = jnp.where(is_lowest, 1, 0)
    pl.when(at_edge)(lambda: rim([open_end], [1 - open_end]))
    pl.when(jnp.logical_not(at_edge))(lambda: rim([0, 1], []))
    for copy in copies:
        copy.wait()


def neighbour_swaps(layers, cores, first):
    pairs = []
    for layer in range(layers):
        partner = layer + 1 if (layer - first) % 2 == 0 else layer - 1
        for core in range(cores):
            here = layer * cores + core
            if 0 <= partner < layers:
                pairs.append((here, partner * cores + (cores - 1 - core if CROSSED[first] else core)))
            else:
                pairs.append((here, layer * cores + cores - 1 - core))
    return pairs


def body(layers, cores, order_parameter, concentration_excess, thermal_subcooling, before, after, flags):
    blocks, side = order_parameter.shape[1], order_parameter.shape[2]
    ring = blocks * cores
    rows = side * ROWS
    f32 = jnp.float32
    before, after, flags = before.T, after.T, flags.T
    owners = [(s * cores + c, s * cores + cores - 1 - c) for s in range(layers) for c in range(cores)]
    fields = [tiles_of(a[0]) for a in (order_parameter, concentration_excess, thermal_subcooling)]
    vmem, hbm = (pl.BlockSpec(memory_space=m) for m in (pltpu.VMEM, pltpu.HBM))
    params = pltpu.CompilerParams(vmem_limit_bytes=VMEM_BYTES)
    message = jax.ShapeDtypeStruct((FIELDS, blocks, EDGE, ROWS, LANES), f32)
    table = pltpu.SMEM(before.shape, jnp.int32)
    in_hbm = lambda *arrays: [pltpu.with_memory_space_constraint(a, pltpu.HBM) for a in arrays]
    numbers = (
        jax.ShapeDtypeStruct((3 * ring + blocks, ROWS, LANES), jnp.int32),
        jax.ShapeDtypeStruct((3 * ring, ROWS, LANES), f32),
    )
    even, odd, own, places, rates = pl.pallas_call(
        functools.partial(pack_kernel, side, blocks, cores, layers),
        out_shape=(message, message, jax.ShapeDtypeStruct((FIELDS, blocks, rows, LANES), f32)) + numbers,
        in_specs=[hbm] * (FIELDS + 3),
        out_specs=(vmem,) * 5,
        scratch_shapes=[table] * 3
        + [pltpu.SemaphoreType.DMA((FIELDS,)), pltpu.SemaphoreType.DMA((3,))],
        compiler_params=params,
        cost_estimate=pl.CostEstimate(flops=0, bytes_accessed=10**6, transcendentals=0),
    )(*in_hbm(*fields, before, after, flags))
    other = lax.ppermute(own, AXES, owners)
    odd_in = lax.ppermute(odd, AXES, neighbour_swaps(layers, cores, 1))
    planes = (FIELDS, ring, side, ROWS, LANES)
    kept = FIELDS + 2
    three = (jax.ShapeDtypeStruct(planes, f32),) * 3
    early = pl.pallas_call(
        functools.partial(early_kernel, side),
        out_shape=three,
        in_specs=[vmem],
        out_specs=(vmem,) * 3,
        compiler_params=params,
        cost_estimate=pl.CostEstimate(flops=0, bytes_accessed=10**6, transcendentals=0),
    )(own)
    even, *early = lax.optimization_barrier((even, *early))
    even_in = lax.ppermute(even, AXES, neighbour_swaps(layers, cores, 0))
    raw, _, _, stepped, ups, downs, face_around = pl.pallas_call(
        functools.partial(first_kernel, side, blocks, cores),
        out_shape=three * 2 + (jax.ShapeDtypeStruct((kept, ring, 2, ROWS, LANES), f32),),
        in_specs=[vmem] * 7,
        out_specs=(vmem,) * 7,
        input_output_aliases={4 + k: k for k in range(3)},
        scratch_shapes=[pltpu.VMEM((kept, ring, side, ROWS, LANES), f32)],
        compiler_params=params,
        cost_estimate=pl.CostEstimate(flops=0, bytes_accessed=10**7, transcendentals=0),
    )(own, other, places, rates, *early)
    odd_in, even_in, stepped = lax.optimization_barrier((odd_in, even_in, stepped))
    arrived = jnp.stack([even_in, odd_in])
    passed_on = lax.ppermute(arrived, AXES, owners)
    result, rim_around = pl.pallas_call(
        functools.partial(second_kernel, side, blocks, cores, layers),
        out_shape=(
            jax.ShapeDtypeStruct((FIELDS, blocks, rows, LANES), f32),
            jax.ShapeDtypeStruct((kept, blocks, 2, ROWS, LANES), f32),
        ),
        in_specs=[vmem] * 7,
        out_specs=(vmem,) * 2,
        scratch_shapes=[
            pltpu.VMEM((4, FIELDS, blocks, side, ROWS, LANES), f32),
            pltpu.VMEM((kept, blocks, side, ROWS, LANES), f32),
            pltpu.VMEM((FIELDS, ring, ROWS, LANES), f32),
        ],
        compiler_params=params,
        cost_estimate=pl.CostEstimate(flops=0, bytes_accessed=10**7, transcendentals=0),
    )(stepped, ups, downs, places, rates, raw, face_around)
    results = pl.pallas_call(
        functools.partial(rim_kernel, side, blocks, cores, layers),
        out_shape=(jax.ShapeDtypeStruct((blocks, rows, LANES), f32),) * FIELDS,
        in_specs=[vmem] * 9,
        out_specs=(hbm,) * FIELDS,
        scratch_shapes=[
            pltpu.VMEM((2, FIELDS, ring, EDGE, ROWS, LANES), f32),
            pltpu.VMEM((2, FIELDS, ring, 2, ROWS, LANES), f32),
            pltpu.VMEM((3, 2, FIELDS, max(ring, 4 * blocks), ROWS, LANES), f32),
            pltpu.VMEM((kept, ring + blocks, 2, ROWS, LANES), f32),
            pltpu.VMEM((FIELDS, 2, blocks, ROWS * ROWS, LANES), f32),
            pltpu.SemaphoreType.DMA((FIELDS, 2)),
            pltpu.SemaphoreType.DMA((FIELDS,)),
        ],
        compiler_params=params,
        cost_estimate=pl.CostEstimate(flops=0, bytes_accessed=10**6, transcendentals=0),
    )(raw, stepped, result, face_around, rim_around, places, rates, arrived, passed_on)
    return tuple(block_of(r, side)[None] for r in results)


def solution(mesh):
    layers, cores = mesh.shape["slab"], mesh.shape["bal"]
    split, copied = P("slab", "bal", None, None), P()
    return jax.shard_map(
        functools.partial(body, layers, cores),
        mesh=mesh,
        in_specs=(split,) * 3 + (copied,) * 3,
        out_specs=(split,) * 3,
        check_vma=False,
    )
```
